128 devices in a mesh: tile: 64 (over z, x, y), mode: 2 (over core).
Axes of the slice: x: 4, y: 4, z: 4, core: 2. Of those that a mesh axis runs over, the one named last changes fastest.
Arguments:
- obj: float32 [64, 2, 384, 384], P('tile'), may hold values from -6 to 6
- probe: float32 [4, 2, 256, 256], P('mode'), may hold values from -3 to 3
- mode_weights: float32 [8, 4], P(None, 'mode'), may hold values from 0.25 to 1
- measured: float32 [256, 256, 256], P('tile'), may hold values from 0 to 4
- corner: int32 [256, 2], P('tile'), may hold values from 0 to 383, as said below
- counts: int32 [64], P('tile'), may hold values from 1 to 4, 128 in all
- weight_index: int32 [256], P('tile'), may hold values from 0 to 7
Outputs:
- obj_new: float32 [64, 2, 384, 384], P('tile')
- probe_new: float32 [4, 2, 256, 256], P('mode')
The draws below stay inside these ranges and needn't reach their ends.
Inputs may be any that keep to these rules, and one draw needn't show every extreme that they name: Tile t has live slots 0 to counts[t] - 1 of its block; the counts sum to 128 and some tile has 4. The first slot of every tile has both corner coordinates between 192 and 320.
All inputs are finite; a program needn't handle non-finite values.
Results may differ from the reference program's by a relative error of at most 0.019.
The reference program's roundings to bfloat16 on the way count: a program that leaves them out, or rounds other values in their place, can miss the bound.
Values may be sent and summed in bfloat16 or wider, within the bound.
A program may use at most 64 MiB of HBM per device.

```python
import math
import jax
import jax.numpy as jnp
import numpy as np
from jax import lax

PATCH = 256
MODES = 4
KINDS = 8
GC = 8
TILE = 384
ITERS = 2
TILE_SLOT_LIMIT = 4
POSITIONS = 128
SLOTS = 256
N_TILE = 64


def draw_corner(key, part):
    first_key, second_key = jax.random.split(jax.random.fold_in(key, 17))
    spread = jax.random.randint(first_key, (SLOTS, 2), 0, TILE, dtype=jnp.int32)
    reaching = jax.random.randint(second_key, (SLOTS, 2), TILE - 3 * PATCH // 4, TILE - PATCH // 4 + 1, dtype=jnp.int32)
    leading = (jnp.arange(SLOTS, dtype=jnp.int32) % TILE_SLOT_LIMIT == 0)[:, None]
    result = jnp.where(leading, reaching, spread)
    result = result.at[1, 0].set(0)
    result = result.at[1, 1].set(TILE - 1)
    return result


def set_ends(values, rng, smallest, largest):
    spot = [jax.random.randint(jax.random.fold_in(rng, axis), (), 0, length) for axis, length in enumerate(values.shape)]
    longest = values.shape.index(max(values.shape))
    beside = spot[:longest] + [(spot[longest] + 1) % values.shape[longest]] + spot[longest + 1:]
    return values.at[tuple(spot)].set(smallest).at[tuple(beside)].set(largest)


def block_scale(rng, dims, pieces, smallest, top_value):
    def one(dim, blocks):
        steps = jax.random.uniform(jax.random.fold_in(jax.random.fold_in(rng, 6), dim), (blocks,), jnp.float32, smallest / len(pieces), top_value / len(pieces))
        return jnp.repeat(jnp.exp(steps), dims[dim] // blocks).reshape((-1,) + (1,) * (len(dims) - dim - 1))

    gain = one(*pieces[0])
    for cut in pieces[1:]:
        gain = gain * one(*cut)
    return gain


def length_profile(number_of, total, most, skew):
    loads = [(1 << 20) // math.isqrt(grade ** skew) + 1 for grade in range(2, number_of + 1)]
    spare, given = total - most - (number_of - 1), [1] * (number_of - 1)
    while spare > 0:
        candidates = [i for i in range(number_of - 1) if given[i] < most]
        mass, remaining = sum([loads[i] for i in candidates]), spare
        for i in candidates:
            more = min(most - given[i], max(1, remaining * loads[i] // mass), spare)
            given[i] = given[i] + more
            spare = spare - more
    return np.array([most] + given)


def uneven(rng, number_of, total, reach, lean):
    if number_of == 2:
        one = jax.random.randint(rng, (), max(1, total - reach), min(reach, total - 1) + 1)
        return jnp.stack([one, total - one])
    tallies = jnp.asarray(length_profile(number_of, total, reach, lean), jnp.int32)
    pairs = (number_of - 1) // 2
    giver, sink = tallies[1:1 + 2 * pairs:2], tallies[2:2 + 2 * pairs:2]
    room = jnp.minimum(giver - 1, reach - sink)
    passed = jax.random.randint(jax.random.fold_in(rng, 1), (pairs,), 0, 1 << 20) % (room + 1)
    tallies = tallies.at[1:1 + 2 * pairs:2].set(giver - passed).at[2:2 + 2 * pairs:2].set(sink + passed)
    return tallies[jax.random.permutation(jax.random.fold_in(rng, 2), number_of)]


def centred(own_key, dims, deviation, bound, pieces=(), held_as=jnp.bfloat16):
    entries = deviation * jax.random.normal(own_key, dims, jnp.float32)
    if pieces:
        entries = entries * block_scale(own_key, dims, pieces, -0.22, 0.18)
    return jnp.clip(entries, -bound, bound).astype(held_as)


def setup_inputs(seed: int = 0) -> dict:
    key_list = jax.random.split(jax.random.key(seed), 8)
    obj = centred(key_list[0], (N_TILE, 2, TILE, TILE), 1.0, 6.0, ((0, 64),), jnp.float32)
    probe = centred(key_list[1], (MODES, 2, PATCH, PATCH), 0.5, 3.0, ((0, 2),), jnp.float32)
    mode_weights = jnp.clip(jnp.exp(math.log(1.0) - 1.3862944 * jax.random.uniform(key_list[2], (KINDS, MODES), jnp.float32) ** block_scale(key_list[2], (KINDS, MODES), ((1, 2),), -0.2, 0.2)), 0.25, 1.0)
    measured = jnp.clip(4.0 * jax.random.uniform(key_list[3], (SLOTS, PATCH, PATCH), jnp.float32) ** block_scale(key_list[3], (SLOTS, PATCH, PATCH), ((0, 64),), -0.2, 0.2), 0.0, 4.0)
    corner = draw_corner(jax.random.fold_in(key_list[7], 71), 0)
    counts = uneven(key_list[5], N_TILE, POSITIONS, TILE_SLOT_LIMIT, 2).astype(jnp.int32)
    weight_index = set_ends(jax.random.randint(key_list[6], (SLOTS,), 0, KINDS), jax.random.fold_in(key_list[6], 1), 0, KINDS - 1).astype(jnp.int32)
    return {"obj": obj, "probe": probe, "mode_weights": mode_weights, "measured": measured, "corner": corner, "counts": counts, "weight_index": weight_index}


def dft_tables(length, sign):
    index = jnp.arange(length, dtype=jnp.int32)
    product = index[:, None] * index[None, :] % length
    angle = product.astype(jnp.float32) * (2.0 * math.pi / length)
    factor = 1.0 / math.sqrt(length)
    real = jnp.cos(angle) * factor
    imag = sign * jnp.sin(angle) * factor
    left = jnp.concatenate([jnp.concatenate([real, -imag], 1), jnp.concatenate([imag, real], 1)], 0).astype(jnp.bfloat16)
    right = jnp.concatenate([real, imag], 1).astype(jnp.bfloat16)
    return (left, right)

def transform(field, tables):
    left, right = tables
    count = field.shape[0]
    length = field.shape[-1]
    first = jnp.einsum('ij,bjk->bik', left.astype(jnp.float32), field.reshape(count, 2 * length, length).astype(jnp.float32))
    first = first.astype(jnp.bfloat16).reshape(count, 2, length, length)
    second = jnp.einsum('bcjk,kl->bcjl', first.astype(jnp.float32), right.astype(jnp.float32))
    real = second[:, 0, :, :length] - second[:, 1, :, length:]
    imag = second[:, 0, :, length:] + second[:, 1, :, :length]
    return jnp.stack([real, imag], 1)

def patch_contributions(object_patches, measured, active_mask, mode_weighting, probe, forward_pass, backward_pass):
    count = object_patches.shape[0]
    modes = probe.shape[0]
    length = probe.shape[-1]
    obj_part = object_patches.astype(jnp.float32)[:, None]
    probe_part = probe[None]
    exit_real = probe_part[:, :, 0] * obj_part[:, :, 0] - probe_part[:, :, 1] * obj_part[:, :, 1]
    exit_imag = probe_part[:, :, 0] * obj_part[:, :, 1] + probe_part[:, :, 1] * obj_part[:, :, 0]
    exit_wave = jnp.stack([exit_real, exit_imag], 2).astype(jnp.bfloat16)
    psi = transform(exit_wave.reshape(count * modes, 2, length, length), forward_pass).reshape(count, modes, 2, length, length)
    power = psi[:, :, 0] * psi[:, :, 0] + psi[:, :, 1] * psi[:, :, 1]
    intensity = lax.optimization_barrier(jnp.sum(mode_weighting[:, :, None, None] * power, 1))
    resid = (intensity - measured) * active_mask[:, None, None]
    scaled = (mode_weighting[:, :, None, None, None] * resid[:, None, None] * psi).astype(jnp.bfloat16)
    chi = transform(scaled.reshape(count * modes, 2, length, length), backward_pass).reshape(count, modes, 2, length, length)
    obj_real = lax.optimization_barrier(jnp.sum(probe_part[:, :, 0] * chi[:, :, 0] + probe_part[:, :, 1] * chi[:, :, 1], 1))
    obj_imag = lax.optimization_barrier(jnp.sum(probe_part[:, :, 0] * chi[:, :, 1] - probe_part[:, :, 1] * chi[:, :, 0], 1))
    probe_real = lax.optimization_barrier(jnp.sum(obj_part[:, :, 0] * chi[:, :, 0] + obj_part[:, :, 1] * chi[:, :, 1], 0))
    probe_imag = lax.optimization_barrier(jnp.sum(obj_part[:, :, 0] * chi[:, :, 1] - obj_part[:, :, 1] * chi[:, :, 0], 0))
    return (jnp.stack([obj_real, obj_imag], 1), jnp.stack([probe_real, probe_imag], 1))

def reference(obj, probe, mode_weights, measured, corner, counts, weight_index):
    forward_pass = dft_tables(PATCH, -1.0)
    backward_pass = dft_tables(PATCH, 1.0)
    zero_index = jnp.zeros((), jnp.int32)
    for sweep in range(ITERS):
        half = obj.astype(jnp.bfloat16)

        def per_tile(carry, tile_id):
            grad_tiles, grad_probe = carry
            beside = (tile_id + 1) % N_TILE
            under = (tile_id + GC) % N_TILE
            diagonal = (tile_id + GC + 1) % N_TILE
            upper = jnp.concatenate([half[tile_id], half[beside][:, :, :PATCH]], 2)
            lower = jnp.concatenate([half[under][:, :PATCH, :], half[diagonal][:, :PATCH, :PATCH]], 2)
            framed = jnp.concatenate([upper, lower], 1)
            corner_start = (tile_id * TILE_SLOT_LIMIT).astype(jnp.int32)
            spots = lax.dynamic_slice_in_dim(corner, corner_start, TILE_SLOT_LIMIT, 0)

            def cut(spot):
                return lax.dynamic_slice(framed, (zero_index, spot[0], spot[1]), (2, PATCH, PATCH))
            object_patches = jax.vmap(cut)(spots)
            measured_amplitudes = lax.dynamic_slice_in_dim(measured, corner_start, TILE_SLOT_LIMIT, 0)
            kinds = lax.dynamic_slice_in_dim(weight_index, corner_start, TILE_SLOT_LIMIT, 0)
            mode_weighting = mode_weights[kinds]
            active_mask = (jnp.arange(TILE_SLOT_LIMIT, dtype=jnp.int32) < counts[tile_id]).astype(jnp.float32)
            object_terms, probe_updates = patch_contributions(object_patches, measured_amplitudes, active_mask, mode_weighting, probe, forward_pass, backward_pass)

            def place(slot, acc):
                where = (zero_index, spots[slot, 0], spots[slot, 1])
                current = lax.dynamic_slice(acc, where, (2, PATCH, PATCH))
                return lax.dynamic_update_slice(acc, current + object_terms[slot], where)
            local = lax.fori_loop(0, TILE_SLOT_LIMIT, place, jnp.zeros((2, TILE + PATCH, TILE + PATCH), jnp.float32))
            grad_tiles = grad_tiles.at[tile_id].add(local[:, :TILE, :TILE])
            grad_tiles = grad_tiles.at[beside, :, :, :PATCH].add(local[:, :TILE, TILE:])
            grad_tiles = grad_tiles.at[under, :, :PATCH, :].add(local[:, TILE:, :TILE])
            grad_tiles = grad_tiles.at[diagonal, :, :PATCH, :PATCH].add(local[:, TILE:, TILE:])
            return ((grad_tiles, grad_probe + probe_updates), None)
        start_tiles = jnp.zeros((N_TILE, 2, TILE, TILE), jnp.float32)
        start_probe = jnp.zeros((MODES, 2, PATCH, PATCH), jnp.float32)
        (grad_tiles, grad_probe), unused = lax.scan(per_tile, (start_tiles, start_probe), jnp.arange(N_TILE, dtype=jnp.int32))
        obj = obj - 0.1 * grad_tiles
        probe = probe - 4.0 / POSITIONS * grad_probe
    return (obj, probe)
```

```python
import functools

import jax
import jax.numpy as jnp
import numpy as np
from jax import lax
from jax.experimental import pallas as pl
from jax.experimental.pallas import tpu as pltpu
from jax.sharding import PartitionSpec as P

MESH = pl.DeviceIdType.MESH
BF16 = jnp.bfloat16
F32 = jnp.float32
GC = 8
ITERS = 2
TILES = 64
SLOTS = 4
MODES = 2
N = 256
L = 128
TILE = 384
FRAME = 640
STEP_OBJECT = 0.1
STEP_PROBE = 4.0 / 128.0


def dft_tables(sign):
    index = np.arange(N, dtype=np.int64)
    angle = (index[:, None] * index[None, :] % N).astype(np.float32) * np.float32(2.0 * np.pi / N)
    factor = np.float32(1.0 / 16.0)
    real = np.cos(angle) * factor
    imag = np.float32(sign) * np.sin(angle) * factor
    left = np.block([[real, -imag], [imag, real]])
    right = np.block([[real, imag], [-imag, real]])
    return jnp.asarray(left, BF16), jnp.asarray(right, BF16)


def kernel(
    obj_ref, probe_ref, mw_ref, meas_ref, corner_ref, counts_ref, widx_ref,
    fl_ref, fr_ref, gl_ref, gr_ref,
    objo_ref, probeo_ref,
    frame, ob, h_right, h_below, h_diag,
    patches, psi, inten, ipart_s, ipart_r, terms, pgrad, zall,
    g_send, g_recv, g_own, margin, m_right, m_below, m_diag,
    rs_send, rs_recv, ag_mine, ag_recv,
    s_halo, r_halo, s_fwd, r_fwd, s_int, r_int, s_g, r_g, s_m, r_m,
    s_rs, r_rs, s_ag, r_ag, s_obj, r_obj,
):
    t = lax.axis_index("tile")
    k = lax.axis_index("mode")
    other = 1 - k

    def away(by):
        return lax.rem(t + (TILES + by) % TILES, TILES)

    def remote(src, dst, ssem, rsem, tile, core):
        return pltpu.make_async_remote_copy(
            src_ref=src, dst_ref=dst, send_sem=ssem, recv_sem=rsem,
            device_id=(tile, core), device_id_type=MESH,
        )

    barrier = pltpu.get_barrier_semaphore()

    def greet(p, _):
        pl.semaphore_signal(barrier, inc=1, device_id=(lax.rem(t + p, TILES), k), device_id_type=MESH)
        return 0

    lax.fori_loop(1, TILES, greet, 0)
    pl.semaphore_signal(barrier, inc=1, device_id=(t, other), device_id_type=MESH)

    probeo_ref[...] = probe_ref[...]
    objo_ref[...] = obj_ref[...]
    for c in range(2):
        for j in range(3):
            ob[c, j] = obj_ref[0, c, :, j * L:(j + 1) * L].astype(BF16)
    zall[0] = jnp.zeros((1024, L), F32)

    def clear(i, _):
        zall[i, 0:TILE] = jnp.zeros((TILE, L), F32)
        zall[i, FRAME:1024] = jnp.zeros((1024 - FRAME, L), F32)
        return 0

    lax.fori_loop(1, 25, clear, 0)
    pl.semaphore_wait(barrier, TILES)

    lane = lax.broadcasted_iota(jnp.int32, (N, L), 1)

    def sweep(it, _):
        halos = (
            (ob.at[k, pl.ds(0, 2)], h_right, away(-1)),
            (ob.at[k, :, pl.ds(0, N)], h_below, away(-GC)),
            (ob.at[k, pl.ds(0, 2), pl.ds(0, N)], h_diag, away(-GC - 1)),
        )
        sends = [
            remote(src, dst.at[k], s_halo.at[i], r_halo.at[i], to, k)
            for i, (src, dst, to) in enumerate(halos)
        ]
        for send in sends:
            send.start()
        forwards = []
        for i, (src, dst, to) in enumerate(halos):
            sends[i].wait()
            forward = remote(dst.at[k], dst.at[k], s_fwd.at[i], r_fwd.at[i], t, other)
            forward.start()
            forwards.append(forward)
        for c in range(2):
            for j in range(3):
                frame[c, j, 0:TILE] = ob[c, j].astype(F32)
        for forward in forwards:
            forward.wait()
        for c in range(2):
            for j in range(2):
                frame[c, 3 + j, 0:TILE] = h_right[c, j].astype(F32)
                frame[c, 3 + j, TILE:FRAME] = h_diag[c, j].astype(F32)
            for j in range(3):
                frame[c, j, TILE:FRAME] = h_below[c, j].astype(F32)

        def intensity_copy(s):
            return remote(ipart_s.at[s], ipart_r.at[s], s_int.at[s], r_int.at[s], t, other)

        def forward_slot(s, _):
            row = corner_ref[s, 0]
            col = corner_ref[s, 1]
            q = lax.div(col, L)
            rem = lax.rem(col, L)
            back = lax.rem(L - rem, L)
            for c in range(2):
                rolled = [
                    pltpu.roll(frame[c, q + j, pl.ds(row, N), :], back, 1) for j in range(3)
                ]
                for j in range(2):
                    patches[s, c, :, j * L:(j + 1) * L] = jnp.where(
                        lane < L - rem, rolled[j], rolled[j + 1]
                    )
            o_re = patches[s, 0]
            o_im = patches[s, 1]
            total = None
            for m in range(MODES):
                p_re = probeo_ref[m, 0]
                p_im = probeo_ref[m, 1]
                e_re = (p_re * o_re - p_im * o_im).astype(BF16)
                e_im = (p_re * o_im + p_im * o_re).astype(BF16)
                first = jnp.dot(
                    fl_ref[...], jnp.concatenate([e_re, e_im], 0), preferred_element_type=F32
                ).astype(BF16)
                first = jnp.concatenate([first[:N], first[N:]], 1)
                wave = jnp.dot(first, fr_ref[...], preferred_element_type=F32)
                psi[s, m] = wave
                w = mw_ref[widx_ref[s], m]
                part = w * (wave[:, :N] * wave[:, :N] + wave[:, N:] * wave[:, N:])
                total = part if total is None else total + part
            inten[s] = total
            ipart_s[s] = total.astype(BF16)
            intensity_copy(s).start()
            return 0

        lax.fori_loop(0, SLOTS, forward_slot, 0)

        def scatter_copy(m, p):
            peer = lax.rem(t + p, TILES)
            return remote(
                rs_send.at[m, pl.ds(peer * 16, 16)], rs_recv.at[m, pl.ds(p * 16, 16)],
                s_rs.at[m], r_rs.at[m], peer, k,
            )

        def gather_copy(m, p):
            peer = lax.rem(t + p, TILES)
            return remote(
                ag_mine.at[m], ag_recv.at[m, pl.ds(t * 16, 16)], s_ag.at[m], r_ag.at[m], peer, k
            )

        for m in range(MODES):
            pgrad[...] = jnp.zeros_like(pgrad)

            def backward_slot(s, _):
                w = mw_ref[widx_ref[s], m]
                if m == 0:
                    intensity_copy(s).wait()
                    live = jnp.where(s < counts_ref[0], 1.0, 0.0).astype(F32)
                    inten[s] = (inten[s] + ipart_r[s].astype(F32) - meas_ref[s]) * live
                factor = w * inten[s]
                s_re = (factor * psi[s, m, :, 0:N]).astype(BF16)
                s_im = (factor * psi[s, m, :, N:2 * N]).astype(BF16)
                first = jnp.dot(
                    gl_ref[...], jnp.concatenate([s_re, s_im], 0), preferred_element_type=F32
                ).astype(BF16)
                first = jnp.concatenate([first[:N], first[N:]], 1)
                chi = jnp.dot(first, gr_ref[...], preferred_element_type=F32)
                c_re = chi[:, :N]
                c_im = chi[:, N:]
                p_re = probeo_ref[m, 0]
                p_im = probeo_ref[m, 1]
                o_re = patches[s, 0]
                o_im = patches[s, 1]
                t_re = p_re * c_re + p_im * c_im
                t_im = p_re * c_im - p_im * c_re
                if m == 0:
                    terms[s, 0] = t_re
                    terms[s, 1] = t_im
                else:
                    terms[s, 0] = terms[s, 0] + t_re
                    terms[s, 1] = terms[s, 1] + t_im
                pgrad[0] = pgrad[0] + o_re * c_re + o_im * c_im
                pgrad[1] = pgrad[1] + o_re * c_im - o_im * c_re
                return 0

            lax.fori_loop(0, SLOTS, backward_slot, 0)
            for c in range(2):
                for j in range(2):
                    rs_send[m, (c * 2 + j) * N:(c * 2 + j + 1) * N] = pgrad[
                        c, :, j * L:(j + 1) * L
                    ].astype(BF16)

            def scatter(p, _):
                scatter_copy(m, p).start()
                return 0

            lax.fori_loop(1, TILES, scatter, 0)

        def spread(s, _):
            rem = lax.rem(corner_ref[s, 1], L)
            for c in range(2):
                left = pltpu.roll(terms[s, c, :, 0:L], rem, 1)
                right = pltpu.roll(terms[s, c, :, L:2 * L], rem, 1)
                base = 1 + (s * 2 + c) * 3
                zall[base, TILE:FRAME] = jnp.where(lane >= rem, left, 0.0)
                zall[base + 1, TILE:FRAME] = jnp.where(lane >= rem, right, left)
                zall[base + 2, TILE:FRAME] = jnp.where(lane >= rem, 0.0, right)
            return 0

        lax.fori_loop(0, SLOTS, spread, 0)

        rows_block = 128

        def place(c, j, b):
            total = None
            for s in range(SLOTS):
                d = j - lax.div(corner_ref[s, 1], L)
                inside = jnp.logical_and(d >= 0, d <= 2)
                index = jnp.where(inside, 1 + (s * 2 + c) * 3 + d, 0)
                start = TILE - corner_ref[s, 0] + b * rows_block
                part = zall[index, pl.ds(start, rows_block), :]
                total = part if total is None else total + part
            return total

        def place_send(i, _):
            j = lax.div(i, 5)
            b = lax.rem(i, 5)
            rows = pl.ds(pl.multiple_of(b * rows_block, rows_block), rows_block)
            g_send[j, rows, :] = place(other, j, b).astype(BF16)
            return 0

        lax.fori_loop(0, 25, place_send, 0)
        pair = remote(g_send, g_recv, s_g, r_g, t, other)
        pair.start()

        def place_own(i, _):
            j = lax.div(i, 5)
            b = lax.rem(i, 5)
            rows = pl.ds(pl.multiple_of(b * rows_block, rows_block), rows_block)
            g_own[j, rows, :] = place(k, j, b)
            return 0

        lax.fori_loop(0, 25, place_own, 0)
        pair.wait()
        for j in range(5):
            total = g_own[j] + g_recv[j].astype(F32)
            g_own[j] = total
            margin[j] = total.astype(BF16)
        margins = (
            (margin.at[pl.ds(3, 2), pl.ds(0, TILE)], m_right, away(1)),
            (margin.at[pl.ds(0, 3), pl.ds(TILE, N)], m_below, away(GC)),
            (margin.at[pl.ds(3, 2), pl.ds(TILE, N)], m_diag, away(GC + 1)),
        )
        sends = [
            remote(src, dst, s_m.at[i], r_m.at[i], to, k)
            for i, (src, dst, to) in enumerate(margins)
        ]
        for send in sends:
            send.start()

        def gather(m):
            whole = remote(
                rs_send.at[m, pl.ds(16, 63 * 16)], rs_recv.at[m, pl.ds(16, 63 * 16)],
                s_rs.at[m], r_rs.at[m], away(1), k,
            )
            whole.wait()
            total = rs_send[m, pl.ds(pl.multiple_of(t * 16, 16), 16), :].astype(F32)
            rest = rs_recv[m, 16:64 * 16].astype(F32).reshape(63, 16, L)
            total = (total + jnp.sum(rest, 0)).astype(BF16)
            ag_mine[m] = total
            ag_recv[m, pl.ds(pl.multiple_of(t * 16, 16), 16), :] = total

            def one(p, _):
                gather_copy(m, p).start()
                return 0

            lax.fori_loop(1, TILES, one, 0)

        for m in range(MODES):
            gather(m)

        for send in sends:
            send.wait()
        for j in range(3):
            total = g_own[j, 0:TILE]
            below = m_below[j].astype(F32)
            if j < 2:
                below = below + m_diag[j].astype(F32)
            total = total + jnp.concatenate([below, jnp.zeros((TILE - N, L), F32)], 0)
            if j < 2:
                total = total + m_right[j].astype(F32)
            now = objo_ref[0, k, :, j * L:(j + 1) * L] - STEP_OBJECT * total
            objo_ref[0, k, :, j * L:(j + 1) * L] = now
            ob[k, j] = now.astype(BF16)
        share = remote(ob.at[k], ob.at[k], s_fwd.at[3], r_fwd.at[3], t, other)
        share.start()

        for m in range(MODES):
            remote(
                rs_send.at[m, pl.ds(16, 63 * 16)], ag_recv.at[m, pl.ds(16, 63 * 16)],
                s_ag.at[m], r_ag.at[m], away(1), k,
            ).wait()
            for c in range(2):
                for j in range(2):
                    grad = ag_recv[m, (c * 2 + j) * N:(c * 2 + j + 1) * N].astype(F32)
                    cols = slice(j * L, (j + 1) * L)
                    probeo_ref[m, c, :, cols] = probeo_ref[m, c, :, cols] - STEP_PROBE * grad
        share.wait()
        return 0

    lax.fori_loop(0, ITERS, sweep, 0)
    last = remote(objo_ref.at[0, k], objo_ref.at[0, k], s_obj, r_obj, t, other)
    last.start()
    last.wait()


def body(obj, probe, mode_weights, measured, corner, counts, weight_index):
    vmem = pl.BlockSpec(memory_space=pltpu.VMEM)
    smem = pl.BlockSpec(memory_space=pltpu.SMEM)
    dma = pltpu.SemaphoreType.DMA
    return pl.pallas_call(
        kernel,
        name="ptycho",
        out_shape=(
            jax.ShapeDtypeStruct(obj.shape, F32),
            jax.ShapeDtypeStruct(probe.shape, F32),
        ),
        in_specs=[vmem, vmem, smem, vmem, smem, smem, smem, vmem, vmem, vmem, vmem],
        out_specs=(vmem, vmem),
        scratch_shapes=[
            pltpu.VMEM((2, 5, FRAME, L), F32),
            pltpu.VMEM((2, 3, TILE, L), BF16),
            pltpu.VMEM((2, 2, TILE, L), BF16),
            pltpu.VMEM((2, 3, N, L), BF16),
            pltpu.VMEM((2, 2, N, L), BF16),
            pltpu.VMEM((SLOTS, 2, N, N), F32),
            pltpu.VMEM((SLOTS, MODES, N, 2 * N), F32),
            pltpu.VMEM((SLOTS, N, N), F32),
            pltpu.VMEM((SLOTS, N, N), BF16),
            pltpu.VMEM((SLOTS, N, N), BF16),
            pltpu.VMEM((SLOTS, 2, N, N), F32),
            pltpu.VMEM((2, N, N), F32),
            pltpu.VMEM((25, 1024, L), F32),
            pltpu.VMEM((5, FRAME, L), BF16),
            pltpu.VMEM((5, FRAME, L), BF16),
            pltpu.VMEM((5, FRAME, L), F32),
            pltpu.VMEM((5, FRAME, L), BF16),
            pltpu.VMEM((2, TILE, L), BF16),
            pltpu.VMEM((3, N, L), BF16),
            pltpu.VMEM((2, N, L), BF16),
            pltpu.VMEM((MODES, 1024, L), BF16),
            pltpu.VMEM((MODES, 1024, L), BF16),
            pltpu.VMEM((MODES, 16, L), BF16),
            pltpu.VMEM((MODES, 1024, L), BF16),
            dma((3,)), dma((3,)), dma((4,)), dma((4,)), dma((4,)), dma((4,)),
            dma, dma, dma((3,)), dma((3,)),
            dma((2,)), dma((2,)), dma((2,)), dma((2,)), dma, dma,
        ],
        compiler_params=pltpu.CompilerParams(
            collective_id=0, has_side_effects=True, vmem_limit_bytes=60 << 20
        ),
    )(obj, probe, mode_weights, measured, corner, counts, weight_index,
      *dft_tables(-1.0), *dft_tables(1.0))


def solution(mesh):
    placed = (
        P("tile", None, None, None),
        P("mode", None, None, None),
        P(None, "mode"),
        P("tile", None, None),
        P("tile", None),
        P("tile"),
        P("tile"),
    )
    return jax.shard_map(
        body,
        mesh=mesh,
        in_specs=placed,
        out_specs=(P("tile", None, None, None), P("mode", None, None, None)),
        check_vma=False,
    )
```

```python
import functools

import jax
import jax.numpy as jnp
import numpy as np
from jax import lax
from jax.experimental import pallas as pl
from jax.experimental.pallas import tpu as pltpu
from jax.sharding import PartitionSpec as P

MESH = pl.DeviceIdType.MESH
BF16 = jnp.bfloat16
F32 = jnp.float32
GC = 8
ITERS = 2
TILES = 64
SLOTS = 4
MODES = 2
N = 256
L = 128
TILE = 384
FRAME = 640
STEP_OBJECT = 0.1
STEP_PROBE = 4.0 / 128.0


def dft_tables():
    index = np.arange(N, dtype=np.int64)
    angle = (index[:, None] * index[None, :] % N).astype(np.float32) * np.float32(2.0 * np.pi / N)
    factor = np.float32(1.0 / 16.0)
    real = np.cos(angle) * factor
    imag = -np.sin(angle) * factor
    one = np.block([[real, -imag], [imag, real]])
    two = np.block([[real, imag], [-imag, real]])
    return jnp.asarray(one, BF16), jnp.asarray(two, BF16)


def kernel(
    obj_hbm, probe_hbm, mw_ref, meas_hbm, corner_ref, counts_ref, widx_ref, one_hbm, two_hbm,
    obj_out, gobj, probe_out, gprobe,
    objs, probes, meas, one, two,
    frame, ob, h_right, h_below, h_diag,
    patches, psi, inten, ipart_s, ipart_r, terms, pgrad, zall,
    g_send, g_recv, g_own, margin, m_right, m_below, m_diag,
    rs_send, rs_recv, ag_mine,
    s_in, s_out, s_halo, r_halo, s_fwd, r_fwd, s_int, r_int, s_g, r_g, s_m, r_m,
    s_rs, r_rs, s_ag, r_ag, s_share, r_share, stage_y, stage_z,
):
    t = lax.axis_index("tile")
    k = lax.axis_index("mode")
    other = 1 - k

    def away(by):
        return lax.rem(t + (TILES + by) % TILES, TILES)

    def along(axis, by):
        size = 4 ** axis
        digit = lax.rem(lax.div(t, size), 4)
        return t + (lax.rem(digit + by, 4) - digit) * size

    def remote(src, dst, ssem, rsem, tile, core):
        return pltpu.make_async_remote_copy(
            src_ref=src, dst_ref=dst, send_sem=ssem, recv_sem=rsem,
            device_id=(tile, core), device_id_type=MESH,
        )

    def signal(sem, tile, core):
        pl.semaphore_signal(sem, inc=1, device_id=(tile, core), device_id_type=MESH)

    loads = [
        pltpu.make_async_copy(src, dst, s_in.at[i])
        for i, (src, dst) in enumerate(
            ((obj_hbm.at[0], objs), (probe_hbm, probes), (one_hbm, one), (two_hbm, two), (meas_hbm, meas))
        )
    ]
    loads[0].start()

    barrier = pltpu.get_barrier_semaphore()
    signal(barrier, t, other)
    for by in (1, GC, GC + 1):
        signal(barrier, away(by), k)
        signal(barrier, away(-by), k)
    for axis in range(3):
        for by in (1, 2, 3):
            signal(barrier, along(axis, by), k)
    for load in loads[1:]:
        load.start()

    loads[0].wait()
    for j in range(3):
        ob[j] = objs[k, :, j * L:(j + 1) * L].astype(BF16)
    pl.semaphore_wait(barrier, 16)

    lane = lax.broadcasted_iota(jnp.int32, (N, L), 1)

    def halo_chunks():
        for j in range(2):
            yield ob.at[j], h_right.at[k, j], away(-1)
        for j in range(3):
            yield ob.at[j, pl.ds(0, N)], h_below.at[k, j], away(-GC)
        for j in range(2):
            yield ob.at[j, pl.ds(0, N)], h_diag.at[k, j], away(-GC - 1)

    halo_sends = [
        remote(src, dst, s_halo.at[i], r_halo.at[i], to, k)
        for i, (src, dst, to) in enumerate(halo_chunks())
    ]
    halo_forwards = [
        remote(dst, dst, s_fwd.at[i], r_fwd.at[i], t, other)
        for i, (src, dst, to) in enumerate(halo_chunks())
    ]
    halo_order = (0, 2, 1, 3, 4, 5, 6)

    def margin_chunks():
        for j in range(2):
            yield margin.at[3 + j, pl.ds(0, TILE)], m_right.at[j], away(1)
        for j in range(3):
            yield margin.at[j, pl.ds(TILE, N)], m_below.at[j], away(GC)
        for j in range(2):
            yield margin.at[3 + j, pl.ds(TILE, N)], m_diag.at[j], away(GC + 1)

    margin_sends = [
        remote(src, dst, s_m.at[i], r_m.at[i], to, k)
        for i, (src, dst, to) in enumerate(margin_chunks())
    ]

    for i in halo_order:
        halo_sends[i].start()

    for by in (1, 2, 3):
        signal(stage_y, along(0, by), k)
    zall[0] = jnp.zeros((1024, L), F32)

    def clear(i, _):
        zall[i, 0:TILE] = jnp.zeros((TILE, L), F32)
        zall[i, FRAME:1024] = jnp.zeros((1024 - FRAME, L), F32)
        return 0

    lax.fori_loop(1, 13, clear, 0)
    pl.semaphore_wait(stage_y, 3)
    for by in (1, 2, 3):
        signal(stage_z, along(2, by), k)
    lax.fori_loop(13, 25, clear, 0)
    pl.semaphore_wait(stage_z, 3)
    for load in loads[1:]:
        load.wait()

    def shard(ref, m, tile):
        return ref.at[
            m, lax.div(tile, 32),
            pl.ds(pl.multiple_of(lax.rem(tile, 16) * 16, 16), 16),
            pl.ds(pl.multiple_of(lax.rem(lax.div(tile, 16), 2) * L, L), L),
        ]

    def sweep(it, _):
        for c in range(2):
            for j in range(3):
                frame[c, j, 0:TILE] = objs[c, :, j * L:(j + 1) * L].astype(BF16).astype(F32)
        for i in halo_order:
            halo_sends[i].wait_recv()
            halo_forwards[i].start()

        def settle(c):
            for j in range(2):
                frame[c, 3 + j, 0:TILE] = h_right[c, j].astype(F32)
            for j in range(3):
                frame[c, j, TILE:FRAME] = h_below[c, j].astype(F32)
            for j in range(2):
                frame[c, 3 + j, TILE:FRAME] = h_diag[c, j].astype(F32)

        settle(k)
        for i in halo_order:
            halo_forwards[i].wait()
        settle(other)
        for send in halo_sends:
            send.wait_send()

        def intensity_copy(s):
            return remote(ipart_s.at[s], ipart_r.at[s], s_int.at[s], r_int.at[s], t, other)

        def forward_slot(s, _):
            row = corner_ref[0, s]
            col = corner_ref[1, s]
            q = lax.div(col, L)
            rem = lax.rem(col, L)
            back = lax.rem(L - rem, L)
            for c in range(2):
                rolled = [
                    pltpu.roll(frame[c, q + j, pl.ds(row, N), :], back, 1) for j in range(3)
                ]
                for j in range(2):
                    patches[s, c, :, j * L:(j + 1) * L] = jnp.where(
                        lane < L - rem, rolled[j], rolled[j + 1]
                    )
            o_re = patches[s, 0]
            o_im = patches[s, 1]
            total = None
            for m in range(MODES):
                p_re = probes[m, 0]
                p_im = probes[m, 1]
                e_re = (p_re * o_re - p_im * o_im).astype(BF16)
                e_im = (p_re * o_im + p_im * o_re).astype(BF16)
                first = jnp.dot(
                    one[...], jnp.concatenate([e_re, e_im], 0), preferred_element_type=F32
                ).astype(BF16)
                first = jnp.concatenate([first[:N], first[N:]], 1)
                wave = jnp.dot(first, two[...], preferred_element_type=F32)
                psi[s, m] = wave
                w = mw_ref[m, widx_ref[s]]
                part = w * (wave[:, :N] * wave[:, :N] + wave[:, N:] * wave[:, N:])
                total = part if total is None else total + part
            inten[s] = total
            ipart_s[s] = total.astype(BF16)
            intensity_copy(s).start()
            return 0

        lax.fori_loop(0, SLOTS, forward_slot, 0)

        def scatter_copy(m, p):
            peer = lax.rem(t + p, TILES)
            return remote(
                shard(rs_send, m, peer), rs_recv.at[m, pl.ds(p * 16, 16)],
                s_rs.at[m], r_rs.at[m], peer, k,
            )

        def gather_copy(m, p):
            peer = lax.rem(t + p, TILES)
            return remote(
                ag_mine.at[m], shard(gprobe, m, t), s_ag.at[m], r_ag.at[m], peer, k
            )

        for m in range(MODES):
            pgrad[...] = jnp.zeros_like(pgrad)

            def backward_slot(s, _):
                w = mw_ref[m, widx_ref[s]]
                if m == 0:
                    intensity_copy(s).wait()
                    live = jnp.where(s < counts_ref[0], 1.0, 0.0).astype(F32)
                    inten[s] = (inten[s] + ipart_r[s].astype(F32) - meas[s]) * live
                factor = w * inten[s]
                s_re = (factor * psi[s, m, :, 0:N]).astype(BF16)
                s_im = (factor * psi[s, m, :, N:2 * N]).astype(BF16)
                first = jnp.dot(
                    two[...], jnp.concatenate([s_re, s_im], 0), preferred_element_type=F32
                ).astype(BF16)
                first = jnp.concatenate([first[:N], first[N:]], 1)
                chi = jnp.dot(first, one[...], preferred_element_type=F32)
                c_re = chi[:, :N]
                c_im = chi[:, N:]
                p_re = probes[m, 0]
                p_im = probes[m, 1]
                o_re = patches[s, 0]
                o_im = patches[s, 1]
                t_re = p_re * c_re + p_im * c_im
                t_im = p_re * c_im - p_im * c_re
                if m == 0:
                    terms[s, 0] = t_re
                    terms[s, 1] = t_im
                else:
                    terms[s, 0] = terms[s, 0] + t_re
                    terms[s, 1] = terms[s, 1] + t_im
                pgrad[0] = pgrad[0] + o_re * c_re + o_im * c_im
                pgrad[1] = pgrad[1] + o_re * c_im - o_im * c_re
                return 0

            lax.fori_loop(0, SLOTS, backward_slot, 0)
            rs_send[m] = pgrad[...].astype(BF16)

            def scatter(p, _):
                scatter_copy(m, p).start()
                return 0

            lax.fori_loop(1, TILES, scatter, 0)

        def spread(s, _):
            rem = lax.rem(corner_ref[1, s], L)
            for c in range(2):
                left = pltpu.roll(terms[s, c, :, 0:L], rem, 1)
                right = pltpu.roll(terms[s, c, :, L:2 * L], rem, 1)
                base = 1 + (s * 2 + c) * 3
                zall[base, TILE:FRAME] = jnp.where(lane >= rem, left, 0.0)
                zall[base + 1, TILE:FRAME] = jnp.where(lane >= rem, right, left)
                zall[base + 2, TILE:FRAME] = jnp.where(lane >= rem, 0.0, right)
            return 0

        lax.fori_loop(0, SLOTS, spread, 0)

        rows_block = 128

        def place(c, j, b):
            total = None
            for s in range(SLOTS):
                d = j - lax.div(corner_ref[1, s], L)
                inside = jnp.logical_and(d >= 0, d <= 2)
                index = jnp.where(inside, 1 + (s * 2 + c) * 3 + d, 0)
                start = TILE - corner_ref[0, s] + b * rows_block
                part = zall[index, pl.ds(start, rows_block), :]
                total = part if total is None else total + part
            return total

        def block(b):
            return pl.ds(pl.multiple_of(b * rows_block, rows_block), rows_block)

        def place_send(i, _):
            j = lax.div(i, 5)
            b = lax.rem(i, 5)
            g_send[j, block(b), :] = place(other, j, b).astype(BF16)
            return 0

        pairs = [
            remote(g_send.at[js], g_recv.at[js], s_g.at[i], r_g.at[i], t, other)
            for i, js in enumerate((pl.ds(3, 2), pl.ds(0, 3)))
        ]
        lax.fori_loop(15, 25, place_send, 0)
        pairs[0].start()
        lax.fori_loop(0, 15, place_send, 0)
        pairs[1].start()

        def place_margin(j, b):
            margin[j, block(b), :] = (
                place(k, j, b) + g_recv[j, block(b), :].astype(F32)
            ).astype(BF16)

        def place_right(i, _):
            place_margin(3 + lax.div(i, 5), lax.rem(i, 5))
            return 0

        def place_below(i, _):
            place_margin(lax.div(i, 2), 3 + lax.rem(i, 2))
            return 0

        def place_tile(i, _):
            j = lax.div(i, 3)
            b = lax.rem(i, 3)
            g_own[j, block(b), :] = place(k, j, b) + g_recv[j, block(b), :].astype(F32)
            return 0

        pairs[0].wait()
        lax.fori_loop(0, 10, place_right, 0)
        for i in (5, 6, 0, 1):
            margin_sends[i].start()
        pairs[1].wait()
        lax.fori_loop(0, 6, place_below, 0)
        for i in (2, 3, 4):
            margin_sends[i].start()
        lax.fori_loop(0, 9, place_tile, 0)

        def gather(m):
            whole = rs_recv.at[m, pl.ds(16, 63 * 16)]
            remote(whole, whole, s_rs.at[m], r_rs.at[m], away(1), k).wait()
            own = shard(rs_send, m, t)[...].astype(F32)
            rest = rs_recv[m, 16:64 * 16].astype(F32).reshape(63, 16, L)
            total = (own + jnp.sum(rest, 0)).astype(BF16)
            ag_mine[m] = total
            shard(gprobe, m, t)[...] = total

            def one_copy(p, _):
                gather_copy(m, p).start()
                return 0

            lax.fori_loop(1, TILES, one_copy, 0)

        for m in range(MODES):
            gather(m)

        for send in margin_sends:
            send.wait()
        more = it < ITERS - 1
        for j in range(3):
            cols = slice(j * L, (j + 1) * L)
            upper = g_own[j, 0:N] + m_below[j].astype(F32)
            lower = g_own[j, N:TILE]
            if j < 2:
                upper = upper + m_diag[j].astype(F32) + m_right[j, 0:N].astype(F32)
                lower = lower + m_right[j, N:TILE].astype(F32)
            gobj[0, k, 0:N, cols] = upper.astype(BF16)
            gobj[0, k, N:TILE, cols] = lower.astype(BF16)
        share = remote(gobj.at[0, k], gobj.at[0, k], s_share, r_share, t, other)
        share.start()

        @pl.when(more)
        def _():
            for j in range(3):
                cols = slice(j * L, (j + 1) * L)
                now = objs[k, :, cols] - STEP_OBJECT * gobj[0, k, :, cols].astype(F32)
                objs[k, :, cols] = now
                ob[j] = now.astype(BF16)
            for i in halo_order:
                halo_sends[i].start()

        for m in range(MODES):
            whole = rs_recv.at[m, pl.ds(16, 63 * 16)]
            remote(whole, whole, s_ag.at[m], r_ag.at[m], away(1), k).wait()
        share.wait()

        @pl.when(more)
        def _():
            probes[...] = probes[...] - STEP_PROBE * gprobe[...].astype(F32)
            objs[other] = objs[other] - STEP_OBJECT * gobj[0, other].astype(F32)
            pltpu.make_async_copy(objs, obj_out.at[0], s_out.at[0]).start()
            pltpu.make_async_copy(probes, probe_out, s_out.at[1]).start()

        return 0

    lax.fori_loop(0, ITERS, sweep, 0)
    pltpu.make_async_copy(objs, obj_out.at[0], s_out.at[0]).wait()
    pltpu.make_async_copy(probes, probe_out, s_out.at[1]).wait()


def body(obj, probe, mode_weights, measured, corner, counts, weight_index):
    vmem = pl.BlockSpec(memory_space=pltpu.VMEM)
    smem = pl.BlockSpec(memory_space=pltpu.SMEM)
    hbm = pl.BlockSpec(memory_space=pl.ANY)
    dma = pltpu.SemaphoreType.DMA
    regular = pltpu.SemaphoreType.REGULAR
    obj_1, grad_obj, probe_1, grad_probe = pl.pallas_call(
        kernel,
        name="ptycho",
        out_shape=(
            jax.ShapeDtypeStruct(obj.shape, F32),
            jax.ShapeDtypeStruct(obj.shape, BF16),
            jax.ShapeDtypeStruct(probe.shape, F32),
            jax.ShapeDtypeStruct(probe.shape, BF16),
        ),
        in_specs=[hbm, hbm, smem, hbm, smem, smem, smem, hbm, hbm],
        out_specs=(hbm, vmem, hbm, vmem),
        scratch_shapes=[
            pltpu.VMEM((2, TILE, TILE), F32),
            pltpu.VMEM((MODES, 2, N, N), F32),
            pltpu.VMEM((SLOTS, N, N), F32),
            pltpu.VMEM((2 * N, 2 * N), BF16),
            pltpu.VMEM((2 * N, 2 * N), BF16),
            pltpu.VMEM((2, 5, FRAME, L), F32),
            pltpu.VMEM((3, TILE, L), BF16),
            pltpu.VMEM((2, 2, TILE, L), BF16),
            pltpu.VMEM((2, 3, N, L), BF16),
            pltpu.VMEM((2, 2, N, L), BF16),
            pltpu.VMEM((SLOTS, 2, N, N), F32),
            pltpu.VMEM((SLOTS, MODES, N, 2 * N), F32),
            pltpu.VMEM((SLOTS, N, N), F32),
            pltpu.VMEM((SLOTS, N, N), BF16),
            pltpu.VMEM((SLOTS, N, N), BF16),
            pltpu.VMEM((SLOTS, 2, N, N), F32),
            pltpu.VMEM((2, N, N), F32),
            pltpu.VMEM((25, 1024, L), F32),
            pltpu.VMEM((5, FRAME, L), BF16),
            pltpu.VMEM((5, FRAME, L), BF16),
            pltpu.VMEM((3, TILE, L), F32),
            pltpu.VMEM((5, FRAME, L), BF16),
            pltpu.VMEM((2, TILE, L), BF16),
            pltpu.VMEM((3, N, L), BF16),
            pltpu.VMEM((2, N, L), BF16),
            pltpu.VMEM((MODES, 2, N, N), BF16),
            pltpu.VMEM((MODES, 1024, L), BF16),
            pltpu.VMEM((MODES, 16, L), BF16),
            dma((5,)), dma((2,)), dma((7,)), dma((7,)), dma((7,)), dma((7,)), dma((4,)), dma((4,)),
            dma((2,)), dma((2,)), dma((7,)), dma((7,)),
            dma((2,)), dma((2,)), dma((2,)), dma((2,)), dma, dma, regular, regular,
        ],
        compiler_params=pltpu.CompilerParams(
            collective_id=0, has_side_effects=True, vmem_limit_bytes=60 << 20
        ),
    )(obj, probe, mode_weights.T, measured, corner.T, counts, weight_index, *dft_tables())
    return (
        obj_1 - STEP_OBJECT * grad_obj.astype(F32),
        probe_1 - STEP_PROBE * grad_probe.astype(F32),
    )


def solution(mesh):
    placed = (
        P("tile", None, None, None),
        P("mode", None, None, None),
        P(None, "mode"),
        P("tile", None, None),
        P("tile", None),
        P("tile"),
        P("tile"),
    )
    return jax.shard_map(
        body,
        mesh=mesh,
        in_specs=placed,
        out_specs=(P("tile", None, None, None), P("mode", None, None, None)),
        check_vma=False,
    )
```

```python
import functools

import jax
import jax.numpy as jnp
import numpy as np
from jax import lax
from jax.experimental import pallas as pl
from jax.experimental.pallas import tpu as pltpu
from jax.sharding import PartitionSpec as P

MESH = pl.DeviceIdType.MESH
BF16 = jnp.bfloat16
F32 = jnp.float32
GC = 8
ITERS = 2
TILES = 64
SLOTS = 4
MODES = 2
N = 256
L = 128
TILE = 384
FRAME = 640
STEP_OBJECT = 0.1
STEP_PROBE = 4.0 / 128.0


def dft_tables():
    index = np.arange(N, dtype=np.int64)
    angle = (index[:, None] * index[None, :] % N).astype(np.float32) * np.float32(2.0 * np.pi / N)
    factor = np.float32(1.0 / 16.0)
    real = np.cos(angle) * factor
    imag = -np.sin(angle) * factor
    one = np.block([[real, -imag], [imag, real]])
    two = np.block([[real, imag], [-imag, real]])
    return jnp.asarray(one, BF16), jnp.asarray(two, BF16)


def transform(fields, left, right):
    stacked = jnp.concatenate([jnp.concatenate(pair, 0) for pair in fields], 1)
    first = jnp.dot(left[...], stacked, preferred_element_type=F32).astype(BF16)
    rows = [
        jnp.concatenate([first[:N, i * N:(i + 1) * N], first[N:, i * N:(i + 1) * N]], 1)
        for i in range(len(fields))
    ]
    second = jnp.dot(jnp.concatenate(rows, 0), right[...], preferred_element_type=F32)
    return [second[i * N:(i + 1) * N] for i in range(len(fields))]


def kernel(
    obj_hbm, probe_hbm, mw_ref, meas_hbm, corner_ref, counts_ref, widx_ref, one_hbm, two_hbm,
    obj_out, gobj, probe_out, gprobe,
    meas, one, two,
    frame, ob, h_right, h_below, h_diag,
    patches, psi, inten, ipart_s, ipart_r, terms, pgrad, zall,
    g_send, g_recv, g_own, margin, m_right, m_below, m_diag,
    rs_send, rs_recv, ag_mine,
    s_in, s_halo, r_halo, s_fwd, r_fwd, s_int, r_int, s_g, r_g, s_m, r_m,
    s_rs, r_rs, s_ag, r_ag, s_share, r_share, stage_y, stage_z,
):
    objs = obj_out.at[0]
    probes = probe_out
    t = lax.axis_index("tile")
    k = lax.axis_index("mode")
    other = 1 - k

    def away(by):
        return lax.rem(t + (TILES + by) % TILES, TILES)

    def along(axis, by):
        size = 4 ** axis
        digit = lax.rem(lax.div(t, size), 4)
        return t + (lax.rem(digit + by, 4) - digit) * size

    def remote(src, dst, ssem, rsem, tile, core):
        return pltpu.make_async_remote_copy(
            src_ref=src, dst_ref=dst, send_sem=ssem, recv_sem=rsem,
            device_id=(tile, core), device_id_type=MESH,
        )

    def signal(sem, tile, core):
        pl.semaphore_signal(sem, inc=1, device_id=(tile, core), device_id_type=MESH)

    loads = [
        pltpu.make_async_copy(src, dst, s_in.at[i])
        for i, (src, dst) in enumerate(
            ((obj_hbm.at[0], objs), (probe_hbm, probes), (one_hbm, one), (two_hbm, two), (meas_hbm, meas))
        )
    ]
    loads[0].start()

    barrier = pltpu.get_barrier_semaphore()
    signal(barrier, t, other)
    for by in (1, GC, GC + 1):
        signal(barrier, away(by), k)
        signal(barrier, away(-by), k)
    for axis in range(3):
        for by in (1, 2, 3):
            signal(barrier, along(axis, by), k)
    for load in loads[1:]:
        load.start()

    loads[0].wait()
    for j in range(3):
        ob[j] = objs[k, :, j * L:(j + 1) * L].astype(BF16)
    pl.semaphore_wait(barrier, 16)

    lane = lax.broadcasted_iota(jnp.int32, (N, L), 1)

    def halo_chunks():
        for j in range(2):
            yield ob.at[j], h_right.at[k, j], away(-1)
        for j in range(3):
            yield ob.at[j, pl.ds(0, N)], h_below.at[k, j], away(-GC)
        for j in range(2):
            yield ob.at[j, pl.ds(0, N)], h_diag.at[k, j], away(-GC - 1)

    halo_sends = [
        remote(src, dst, s_halo.at[i], r_halo.at[i], to, k)
        for i, (src, dst, to) in enumerate(halo_chunks())
    ]
    halo_forwards = [
        remote(dst, dst, s_fwd.at[i], r_fwd.at[i], t, other)
        for i, (src, dst, to) in enumerate(halo_chunks())
    ]
    halo_order = (5, 6, 2, 3, 4, 0, 1)

    def margin_chunks():
        for j in range(2):
            yield margin.at[3 + j, pl.ds(0, TILE)], m_right.at[j], away(1)
        for j in range(3):
            yield margin.at[j, pl.ds(TILE, N)], m_below.at[j], away(GC)
        for j in range(2):
            yield margin.at[3 + j, pl.ds(TILE, N)], m_diag.at[j], away(GC + 1)

    margin_sends = [
        remote(src, dst, s_m.at[i], r_m.at[i], to, k)
        for i, (src, dst, to) in enumerate(margin_chunks())
    ]

    for i in halo_order:
        halo_sends[i].start()

    for by in (1, 2, 3):
        signal(stage_y, along(0, by), k)
    zall[0] = jnp.zeros((1024, L), F32)

    def clear(i, _):
        zall[i, 0:TILE] = jnp.zeros((TILE, L), F32)
        zall[i, FRAME:1024] = jnp.zeros((1024 - FRAME, L), F32)
        return 0

    lax.fori_loop(1, 13, clear, 0)
    pl.semaphore_wait(stage_y, 3)
    for by in (1, 2, 3):
        signal(stage_z, along(2, by), k)
    lax.fori_loop(13, 25, clear, 0)
    pl.semaphore_wait(stage_z, 3)
    for load in loads[1:]:
        load.wait()

    def shard(ref, m, tile):
        return ref.at[
            m, lax.div(tile, 32),
            pl.ds(pl.multiple_of(lax.rem(tile, 16) * 16, 16), 16),
            pl.ds(pl.multiple_of(lax.rem(lax.div(tile, 16), 2) * L, L), L),
        ]

    def sweep(it, _):
        for c in range(2):
            for j in range(3):
                frame[c, j, 0:TILE] = objs[c, :, j * L:(j + 1) * L].astype(BF16).astype(F32)
        for i in halo_order:
            halo_sends[i].wait_recv()
            halo_forwards[i].start()

        def settle(c):
            for j in range(2):
                frame[c, 3 + j, 0:TILE] = h_right[c, j].astype(F32)
            for j in range(3):
                frame[c, j, TILE:FRAME] = h_below[c, j].astype(F32)
            for j in range(2):
                frame[c, 3 + j, TILE:FRAME] = h_diag[c, j].astype(F32)

        settle(k)
        for i in halo_order:
            halo_forwards[i].wait()
        settle(other)
        for send in halo_sends:
            send.wait_send()

        def intensity_copy(s):
            return remote(ipart_s.at[s], ipart_r.at[s], s_int.at[s], r_int.at[s], t, other)

        def forward_slot(s):
            row = corner_ref[0, s]
            col = corner_ref[1, s]
            q = lax.div(col, L)
            rem = lax.rem(col, L)
            back = lax.rem(L - rem, L)
            for c in range(2):
                rolled = [
                    pltpu.roll(frame[c, q + j, pl.ds(row, N), :], back, 1) for j in range(3)
                ]
                for j in range(2):
                    patches[s, c, :, j * L:(j + 1) * L] = jnp.where(
                        lane < L - rem, rolled[j], rolled[j + 1]
                    )
            o_re = patches[s, 0]
            o_im = patches[s, 1]
            fields = []
            for m in range(MODES):
                p_re = probes[m, 0]
                p_im = probes[m, 1]
                e_re = (p_re * o_re - p_im * o_im).astype(BF16)
                e_im = (p_re * o_im + p_im * o_re).astype(BF16)
                fields.append((e_re, e_im))
            total = None
            for m, wave in enumerate(transform(fields, one, two)):
                psi[s, m] = wave
                w = mw_ref[m, widx_ref[s]]
                part = w * (wave[:, :N] * wave[:, :N] + wave[:, N:] * wave[:, N:])
                total = part if total is None else total + part
            inten[s] = total
            ipart_s[s] = total.astype(BF16)
            intensity_copy(s).start()

        def forward_pair(i, _):
            forward_slot(2 * i)
            forward_slot(2 * i + 1)
            return 0

        lax.fori_loop(0, SLOTS // 2, forward_pair, 0)

        def scatter_copy(m, p):
            peer = lax.rem(t + p, TILES)
            return remote(
                shard(rs_send, m, peer), rs_recv.at[m, pl.ds(p * 16, 16)],
                s_rs.at[m], r_rs.at[m], peer, k,
            )

        def gather_copy(m, p):
            peer = lax.rem(t + p, TILES)
            return remote(
                ag_mine.at[m], shard(gprobe, m, t), s_ag.at[m], r_ag.at[m], peer, k
            )

        for m in range(MODES):
            pgrad[...] = jnp.zeros_like(pgrad)

            def backward_pair(i):
                fields = []
                for s in (2 * i, 2 * i + 1):
                    w = mw_ref[m, widx_ref[s]]
                    if m == 0:
                        intensity_copy(s).wait()
                        live = jnp.where(s < counts_ref[0], 1.0, 0.0).astype(F32)
                        inten[s] = (inten[s] + ipart_r[s].astype(F32) - meas[s]) * live
                    factor = w * inten[s]
                    s_re = (factor * psi[s, m, :, 0:N]).astype(BF16)
                    s_im = (factor * psi[s, m, :, N:2 * N]).astype(BF16)
                    fields.append((s_re, s_im))
                p_re = probes[m, 0]
                p_im = probes[m, 1]
                for s, chi in zip((2 * i, 2 * i + 1), transform(fields, two, one)):
                    c_re = chi[:, :N]
                    c_im = chi[:, N:]
                    o_re = patches[s, 0]
                    o_im = patches[s, 1]
                    t_re = p_re * c_re + p_im * c_im
                    t_im = p_re * c_im - p_im * c_re
                    if m == 0:
                        terms[s, 0] = t_re
                        terms[s, 1] = t_im
                    else:
                        terms[s, 0] = terms[s, 0] + t_re
                        terms[s, 1] = terms[s, 1] + t_im
                    pgrad[0] = pgrad[0] + o_re * c_re + o_im * c_im
                    pgrad[1] = pgrad[1] + o_re * c_im - o_im * c_re

            def backward_step(i, _):
                backward_pair(i)
                return 0

            lax.fori_loop(0, SLOTS // 2, backward_step, 0)
            rs_send[m] = pgrad[...].astype(BF16)

            def scatter(p, _):
                scatter_copy(m, p).start()
                return 0

            lax.fori_loop(1, TILES, scatter, 0, unroll=9)

        def spread(s, _):
            rem = lax.rem(corner_ref[1, s], L)
            for c in range(2):
                left = pltpu.roll(terms[s, c, :, 0:L], rem, 1)
                right = pltpu.roll(terms[s, c, :, L:2 * L], rem, 1)
                base = 1 + (s * 2 + c) * 3
                zall[base, TILE:FRAME] = jnp.where(lane >= rem, left, 0.0)
                zall[base + 1, TILE:FRAME] = jnp.where(lane >= rem, right, left)
                zall[base + 2, TILE:FRAME] = jnp.where(lane >= rem, 0.0, right)
            return 0

        lax.fori_loop(0, SLOTS, spread, 0)

        rows_block = 128

        def place(c, j, b):
            total = None
            for s in range(SLOTS):
                d = j - lax.div(corner_ref[1, s], L)
                inside = jnp.logical_and(d >= 0, d <= 2)
                index = jnp.where(inside, 1 + (s * 2 + c) * 3 + d, 0)
                start = TILE - corner_ref[0, s] + b * rows_block
                part = zall[index, pl.ds(start, rows_block), :]
                total = part if total is None else total + part
            return total

        def block(b):
            return pl.ds(pl.multiple_of(b * rows_block, rows_block), rows_block)

        def place_send(i, _):
            j = lax.div(i, 5)
            b = lax.rem(i, 5)
            g_send[j, block(b), :] = place(other, j, b).astype(BF16)
            return 0

        pairs = [
            remote(g_send.at[js], g_recv.at[js], s_g.at[i], r_g.at[i], t, other)
            for i, js in enumerate((pl.ds(3, 2), pl.ds(0, 3)))
        ]
        lax.fori_loop(15, 25, place_send, 0)
        pairs[0].start()
        lax.fori_loop(0, 15, place_send, 0)
        pairs[1].start()

        def place_margin(j, b):
            margin[j, block(b), :] = (
                place(k, j, b) + g_recv[j, block(b), :].astype(F32)
            ).astype(BF16)

        def place_right(i, _):
            place_margin(3 + lax.div(i, 5), lax.rem(i, 5))
            return 0

        def place_below(i, _):
            place_margin(lax.div(i, 2), 3 + lax.rem(i, 2))
            return 0

        def place_tile(i, _):
            j = lax.div(i, 3)
            b = lax.rem(i, 3)
            g_own[j, block(b), :] = place(k, j, b) + g_recv[j, block(b), :].astype(F32)
            return 0

        pairs[0].wait()
        lax.fori_loop(0, 10, place_right, 0)
        for i in (5, 6, 0, 1):
            margin_sends[i].start()
        pairs[1].wait()
        lax.fori_loop(0, 6, place_below, 0)
        for i in (2, 3, 4):
            margin_sends[i].start()
        lax.fori_loop(0, 9, place_tile, 0)

        def gather(m):
            whole = rs_recv.at[m, pl.ds(16, 63 * 16)]
            remote(whole, whole, s_rs.at[m], r_rs.at[m], away(1), k).wait()
            own = shard(rs_send, m, t)[...].astype(F32)
            rest = rs_recv[m, 16:64 * 16].astype(F32).reshape(63, 16, L)
            total = (own + jnp.sum(rest, 0)).astype(BF16)
            ag_mine[m] = total
            shard(gprobe, m, t)[...] = total

            def one_copy(p, _):
                gather_copy(m, p).start()
                return 0

            lax.fori_loop(1, TILES, one_copy, 0, unroll=9)

        for m in range(MODES):
            gather(m)

        for send in margin_sends:
            send.wait()
        more = it < ITERS - 1
        for j in range(3):
            cols = slice(j * L, (j + 1) * L)
            upper = g_own[j, 0:N] + m_below[j].astype(F32)
            lower = g_own[j, N:TILE]
            if j < 2:
                upper = upper + m_diag[j].astype(F32) + m_right[j, 0:N].astype(F32)
                lower = lower + m_right[j, N:TILE].astype(F32)
            gobj[0, k, 0:N, cols] = upper.astype(BF16)
            gobj[0, k, N:TILE, cols] = lower.astype(BF16)
        share = remote(gobj.at[0, k], gobj.at[0, k], s_share, r_share, t, other)
        share.start()

        @pl.when(more)
        def _():
            for j in range(3):
                cols = slice(j * L, (j + 1) * L)
                now = objs[k, :, cols] - STEP_OBJECT * gobj[0, k, :, cols].astype(F32)
                objs[k, :, cols] = now
                ob[j] = now.astype(BF16)
            for i in halo_order:
                halo_sends[i].start()

        for m in range(MODES):
            whole = rs_recv.at[m, pl.ds(16, 63 * 16)]
            remote(whole, whole, s_ag.at[m], r_ag.at[m], away(1), k).wait()
        share.wait()

        @pl.when(more)
        def _():
            probes[...] = probes[...] - STEP_PROBE * gprobe[...].astype(F32)
            objs[other] = objs[other] - STEP_OBJECT * gobj[0, other].astype(F32)

        return 0

    lax.fori_loop(0, ITERS, sweep, 0)


def body(obj, probe, mode_weights, measured, corner, counts, weight_index):
    vmem = pl.BlockSpec(memory_space=pltpu.VMEM)
    smem = pl.BlockSpec(memory_space=pltpu.SMEM)
    hbm = pl.BlockSpec(memory_space=pl.ANY)
    dma = pltpu.SemaphoreType.DMA
    regular = pltpu.SemaphoreType.REGULAR
    obj_1, grad_obj, probe_1, grad_probe = pl.pallas_call(
        kernel,
        name="ptycho",
        out_shape=(
            pltpu.VMEM(obj.shape, F32),
            pltpu.VMEM(obj.shape, BF16),
            pltpu.VMEM(probe.shape, F32),
            pltpu.VMEM(probe.shape, BF16),
        ),
        in_specs=[hbm, hbm, smem, hbm, smem, smem, smem, hbm, hbm],
        out_specs=(vmem, vmem, vmem, vmem),
        scratch_shapes=[
            pltpu.VMEM((SLOTS, N, N), F32),
            pltpu.VMEM((2 * N, 2 * N), BF16),
            pltpu.VMEM((2 * N, 2 * N), BF16),
            pltpu.VMEM((2, 5, FRAME, L), F32),
            pltpu.VMEM((3, TILE, L), BF16),
            pltpu.VMEM((2, 2, TILE, L), BF16),
            pltpu.VMEM((2, 3, N, L), BF16),
            pltpu.VMEM((2, 2, N, L), BF16),
            pltpu.VMEM((SLOTS, 2, N, N), F32),
            pltpu.VMEM((SLOTS, MODES, N, 2 * N), F32),
            pltpu.VMEM((SLOTS, N, N), F32),
            pltpu.VMEM((SLOTS, N, N), BF16),
            pltpu.VMEM((SLOTS, N, N), BF16),
            pltpu.VMEM((SLOTS, 2, N, N), F32),
            pltpu.VMEM((2, N, N), F32),
            pltpu.VMEM((25, 1024, L), F32),
            pltpu.VMEM((5, FRAME, L), BF16),
            pltpu.VMEM((5, FRAME, L), BF16),
            pltpu.VMEM((3, TILE, L), F32),
            pltpu.VMEM((5, FRAME, L), BF16),
            pltpu.VMEM((2, TILE, L), BF16),
            pltpu.VMEM((3, N, L), BF16),
            pltpu.VMEM((2, N, L), BF16),
            pltpu.VMEM((MODES, 2, N, N), BF16),
            pltpu.VMEM((MODES, 1024, L), BF16),
            pltpu.VMEM((MODES, 16, L), BF16),
            dma((5,)), dma((7,)), dma((7,)), dma((7,)), dma((7,)), dma((4,)), dma((4,)),
            dma((2,)), dma((2,)), dma((7,)), dma((7,)),
            dma((2,)), dma((2,)), dma((2,)), dma((2,)), dma, dma, regular, regular,
        ],
        compiler_params=pltpu.CompilerParams(
            collective_id=0, has_side_effects=True, vmem_limit_bytes=54 << 20
        ),
    )(obj, probe, mode_weights.T, measured, corner.T, counts, weight_index, *dft_tables())
    return (
        obj_1 - STEP_OBJECT * grad_obj.astype(F32),
        probe_1 - STEP_PROBE * grad_probe.astype(F32),
    )


def solution(mesh):
    placed = (
        P("tile", None, None, None),
        P("mode", None, None, None),
        P(None, "mode"),
        P("tile", None, None),
        P("tile", None),
        P("tile"),
        P("tile"),
    )
    return jax.shard_map(
        body,
        mesh=mesh,
        in_specs=placed,
        out_specs=(P("tile", None, None, None), P("mode", None, None, None)),
        check_vma=False,
    )
```

```python
import functools

import jax
import jax.numpy as jnp
import numpy as np
from jax import lax
from jax.experimental import pallas as pl
from jax.experimental.pallas import tpu as pltpu
from jax.sharding import PartitionSpec as P

MESH = pl.DeviceIdType.MESH
BF16 = jnp.bfloat16
F32 = jnp.float32
GC = 8
ITERS = 2
TILES = 64
SLOTS = 4
MODES = 2
N = 256
L = 128
TILE = 384
FRAME = 640
STEP_OBJECT = 0.1
STEP_PROBE = 4.0 / 128.0


def dft_tables():
    index = np.arange(N, dtype=np.int64)
    angle = (index[:, None] * index[None, :] % N).astype(np.float32) * np.float32(2.0 * np.pi / N)
    factor = np.float32(1.0 / 16.0)
    real = np.cos(angle) * factor
    imag = -np.sin(angle) * factor
    one = np.block([[real, -imag], [imag, real]])
    two = np.block([[real, imag], [-imag, real]])
    return jnp.asarray(one, BF16), jnp.asarray(two, BF16)


def transform(fields, left, right):
    stacked = jnp.concatenate([jnp.concatenate(pair, 0) for pair in fields], 1)
    first = jnp.dot(left[...], stacked, preferred_element_type=F32).astype(BF16)
    rows = [
        jnp.concatenate([first[:N, i * N:(i + 1) * N], first[N:, i * N:(i + 1) * N]], 1)
        for i in range(len(fields))
    ]
    second = jnp.dot(jnp.concatenate(rows, 0), right[...], preferred_element_type=F32)
    return [second[i * N:(i + 1) * N] for i in range(len(fields))]


def kernel(
    obj_hbm, probe_hbm, mw_ref, meas_hbm, corner_ref, counts_ref, widx_ref, one_hbm, two_hbm,
    obj_out, gobj, probe_out, gprobe,
    meas, one, two,
    frame, ob, h_right, h_below, h_diag,
    patches, psi, inten, ipart_s, ipart_r, terms, pgrad, zall,
    g_send, g_recv, g_own, margin, m_right, m_below, m_diag,
    rs_send, rs_recv, ag_mine,
    s_in, s_halo, r_halo, s_fwd, r_fwd, s_int, r_int, s_g, r_g, s_m, r_m,
    s_rs, r_rs, s_ag, r_ag, s_share, r_share, stage_y, stage_z,
):
    objs = obj_out.at[0]
    probes = probe_out
    t = lax.axis_index("tile")
    k = lax.axis_index("mode")
    other = 1 - k

    def away(by):
        return lax.rem(t + (TILES + by) % TILES, TILES)

    def along(axis, by):
        size = 4 ** axis
        digit = lax.rem(lax.div(t, size), 4)
        return t + (lax.rem(digit + by, 4) - digit) * size

    def remote(src, dst, ssem, rsem, tile, core):
        return pltpu.make_async_remote_copy(
            src_ref=src, dst_ref=dst, send_sem=ssem, recv_sem=rsem,
            device_id=(tile, core), device_id_type=MESH,
        )

    def signal(sem, tile, core):
        pl.semaphore_signal(sem, inc=1, device_id=(tile, core), device_id_type=MESH)

    loads = [
        pltpu.make_async_copy(src, dst, s_in.at[i])
        for i, (src, dst) in enumerate(
            ((obj_hbm.at[0], objs), (probe_hbm, probes), (one_hbm, one), (two_hbm, two), (meas_hbm, meas))
        )
    ]
    loads[0].start()

    barrier = pltpu.get_barrier_semaphore()
    signal(barrier, t, other)
    for by in (1, GC, GC + 1):
        signal(barrier, away(by), k)
        signal(barrier, away(-by), k)
    for axis in range(3):
        for by in (1, 2, 3):
            signal(barrier, along(axis, by), k)
    for load in loads[1:]:
        load.start()

    loads[0].wait()
    for j in range(3):
        ob[j] = objs[k, :, j * L:(j + 1) * L].astype(BF16)
    pl.semaphore_wait(barrier, 16)

    lane = lax.broadcasted_iota(jnp.int32, (N, L), 1)

    def halo_chunks():
        for j in range(2):
            yield ob.at[j], h_right.at[k, j], away(-1)
        for j in range(3):
            yield ob.at[j, pl.ds(0, N)], h_below.at[k, j], away(-GC)
        for j in range(2):
            yield ob.at[j, pl.ds(0, N)], h_diag.at[k, j], away(-GC - 1)

    halo_sends = [
        remote(src, dst, s_halo.at[i], r_halo.at[i], to, k)
        for i, (src, dst, to) in enumerate(halo_chunks())
    ]
    halo_forwards = [
        remote(dst, dst, s_fwd.at[i], r_fwd.at[i], t, other)
        for i, (src, dst, to) in enumerate(halo_chunks())
    ]
    halo_order = (5, 6, 2, 3, 4, 0, 1)

    def margin_chunks():
        for j in range(2):
            yield margin.at[3 + j, pl.ds(0, TILE)], m_right.at[j], away(1)
        for j in range(3):
            yield margin.at[j, pl.ds(TILE, N)], m_below.at[j], away(GC)
        for j in range(2):
            yield margin.at[3 + j, pl.ds(TILE, N)], m_diag.at[j], away(GC + 1)

    margin_sends = [
        remote(src, dst, s_m.at[i], r_m.at[i], to, k)
        for i, (src, dst, to) in enumerate(margin_chunks())
    ]

    for i in halo_order:
        halo_sends[i].start()

    for by in (1, 2, 3):
        signal(stage_y, along(0, by), k)
    zall[0] = jnp.zeros((1024, L), F32)

    def clear(i, _):
        zall[i, 0:TILE] = jnp.zeros((TILE, L), F32)
        zall[i, FRAME:1024] = jnp.zeros((1024 - FRAME, L), F32)
        return 0

    lax.fori_loop(1, 13, clear, 0)
    pl.semaphore_wait(stage_y, 3)
    for by in (1, 2, 3):
        signal(stage_z, along(2, by), k)
    lax.fori_loop(13, 25, clear, 0)
    pl.semaphore_wait(stage_z, 3)
    for load in loads[1:]:
        load.wait()

    def shard(ref, m, tile):
        return ref.at[
            m, lax.div(tile, 32),
            pl.ds(pl.multiple_of(lax.rem(tile, 16) * 16, 16), 16),
            pl.ds(pl.multiple_of(lax.rem(lax.div(tile, 16), 2) * L, L), L),
        ]

    def sweep(it, _):
        for c in range(2):
            for j in range(3):
                frame[c, j, 0:TILE] = objs[c, :, j * L:(j + 1) * L].astype(BF16).astype(F32)
        for i in halo_order:
            halo_sends[i].wait_recv()
            halo_forwards[i].start()

        def settle(c):
            for j in range(2):
                frame[c, 3 + j, 0:TILE] = h_right[c, j].astype(F32)
            for j in range(3):
                frame[c, j, TILE:FRAME] = h_below[c, j].astype(F32)
            for j in range(2):
                frame[c, 3 + j, TILE:FRAME] = h_diag[c, j].astype(F32)

        settle(k)
        for i in halo_order:
            halo_forwards[i].wait()
        settle(other)
        for send in halo_sends:
            send.wait_send()

        def intensity_copy(s):
            return remote(ipart_s.at[s], ipart_r.at[s], s_int.at[s], r_int.at[s], t, other)

        def forward_slot(s):
            row = corner_ref[0, s]
            col = corner_ref[1, s]
            q = lax.div(col, L)
            rem = lax.rem(col, L)
            back = lax.rem(L - rem, L)
            for c in range(2):
                rolled = [
                    pltpu.roll(frame[c, q + j, pl.ds(row, N), :], back, 1) for j in range(3)
                ]
                for j in range(2):
                    patches[s, c, :, j * L:(j + 1) * L] = jnp.where(
                        lane < L - rem, rolled[j], rolled[j + 1]
                    )
            o_re = patches[s, 0]
            o_im = patches[s, 1]
            fields = []
            for m in range(MODES):
                p_re = probes[m, 0]
                p_im = probes[m, 1]
                e_re = (p_re * o_re - p_im * o_im).astype(BF16)
                e_im = (p_re * o_im + p_im * o_re).astype(BF16)
                fields.append((e_re, e_im))
            total = None
            for m, wave in enumerate(transform(fields, one, two)):
                psi[s, m] = wave
                w = mw_ref[m, widx_ref[s]]
                part = w * (wave[:, :N] * wave[:, :N] + wave[:, N:] * wave[:, N:])
                total = part if total is None else total + part
            inten[s] = total
            ipart_s[s] = total.astype(BF16)
            intensity_copy(s).start()

        def forward_pair(i, _):
            forward_slot(2 * i)
            forward_slot(2 * i + 1)
            return 0

        lax.fori_loop(0, SLOTS // 2, forward_pair, 0)

        def scatter_copy(m, p):
            peer = lax.rem(t + p, TILES)
            return remote(
                shard(rs_send, m, peer), rs_recv.at[m, pl.ds(p * 16, 16)],
                s_rs.at[m], r_rs.at[m], peer, k,
            )

        def gather_copy(m, p):
            peer = lax.rem(t + p, TILES)
            return remote(
                ag_mine.at[m], shard(gprobe, m, t), s_ag.at[m], r_ag.at[m], peer, k
            )

        for m in range(MODES):
            pgrad[...] = jnp.zeros_like(pgrad)

            def backward_pair(i):
                fields = []
                for s in (2 * i, 2 * i + 1):
                    w = mw_ref[m, widx_ref[s]]
                    if m == 0:
                        intensity_copy(s).wait()
                        live = jnp.where(s < counts_ref[0], 1.0, 0.0).astype(F32)
                        inten[s] = (inten[s] + ipart_r[s].astype(F32) - meas[s]) * live
                    factor = w * inten[s]
                    s_re = (factor * psi[s, m, :, 0:N]).astype(BF16)
                    s_im = (factor * psi[s, m, :, N:2 * N]).astype(BF16)
                    fields.append((s_re, s_im))
                p_re = probes[m, 0]
                p_im = probes[m, 1]
                for s, chi in zip((2 * i, 2 * i + 1), transform(fields, two, one)):
                    c_re = chi[:, :N]
                    c_im = chi[:, N:]
                    o_re = patches[s, 0]
                    o_im = patches[s, 1]
                    t_re = p_re * c_re + p_im * c_im
                    t_im = p_re * c_im - p_im * c_re
                    if m == 0:
                        terms[s, 0] = t_re
                        terms[s, 1] = t_im
                    else:
                        terms[s, 0] = terms[s, 0] + t_re
                        terms[s, 1] = terms[s, 1] + t_im
                    pgrad[0] = pgrad[0] + o_re * c_re + o_im * c_im
                    pgrad[1] = pgrad[1] + o_re * c_im - o_im * c_re

            def backward_step(i, _):
                backward_pair(i)
                return 0

            lax.fori_loop(0, SLOTS // 2, backward_step, 0)
            rs_send[m] = pgrad[...].astype(BF16)

            def scatter(p, _):
                scatter_copy(m, p).start()
                return 0

            lax.fori_loop(1, TILES, scatter, 0, unroll=9)

        def spread(s, _):
            rem = lax.rem(corner_ref[1, s], L)
            for c in range(2):
                left = pltpu.roll(terms[s, c, :, 0:L], rem, 1)
                right = pltpu.roll(terms[s, c, :, L:2 * L], rem, 1)
                base = 1 + (s * 2 + c) * 3
                zall[base, TILE:FRAME] = jnp.where(lane >= rem, left, 0.0)
                zall[base + 1, TILE:FRAME] = jnp.where(lane >= rem, right, left)
                zall[base + 2, TILE:FRAME] = jnp.where(lane >= rem, 0.0, right)
            return 0

        lax.fori_loop(0, SLOTS, spread, 0)

        rows_block = 128

        def place(c, j, b):
            total = None
            for s in range(SLOTS):
                d = j - lax.div(corner_ref[1, s], L)
                inside = jnp.logical_and(d >= 0, d <= 2)
                index = jnp.where(inside, 1 + (s * 2 + c) * 3 + d, 0)
                start = TILE - corner_ref[0, s] + b * rows_block
                part = zall[index, pl.ds(start, rows_block), :]
                total = part if total is None else total + part
            return total

        def block(b):
            return pl.ds(pl.multiple_of(b * rows_block, rows_block), rows_block)

        def place_send(i, _):
            j = lax.div(i, 5)
            b = lax.rem(i, 5)
            g_send[j, block(b), :] = place(other, j, b).astype(BF16)
            return 0

        pairs = [
            remote(g_send.at[js], g_recv.at[js], s_g.at[i], r_g.at[i], t, other)
            for i, js in enumerate((pl.ds(3, 2), pl.ds(0, 3)))
        ]
        lax.fori_loop(15, 25, place_send, 0)
        pairs[0].start()
        lax.fori_loop(0, 15, place_send, 0)
        pairs[1].start()

        def place_margin(j, b):
            margin[j, block(b), :] = (
                place(k, j, b) + g_recv[j, block(b), :].astype(F32)
            ).astype(BF16)

        def place_right(i, _):
            place_margin(3 + lax.div(i, 5), lax.rem(i, 5))
            return 0

        def place_below(i, _):
            place_margin(lax.div(i, 2), 3 + lax.rem(i, 2))
            return 0

        def place_tile(i, _):
            j = lax.div(i, 3)
            b = lax.rem(i, 3)
            g_own[j, block(b), :] = place(k, j, b) + g_recv[j, block(b), :].astype(F32)
            return 0

        pairs[0].wait()
        lax.fori_loop(0, 10, place_right, 0)
        for i in (5, 6, 0, 1):
            margin_sends[i].start()
        pairs[1].wait()
        lax.fori_loop(0, 6, place_below, 0)
        for i in (2, 3, 4):
            margin_sends[i].start()
        lax.fori_loop(0, 9, place_tile, 0)

        def gather(m):
            whole = rs_recv.at[m, pl.ds(16, 63 * 16)]
            remote(whole, whole, s_rs.at[m], r_rs.at[m], away(1), k).wait()
            own = shard(rs_send, m, t)[...].astype(F32)
            rest = rs_recv[m, 16:64 * 16].astype(F32).reshape(63, 16, L)
            total = (own + jnp.sum(rest, 0)).astype(BF16)
            ag_mine[m] = total
            shard(gprobe, m, t)[...] = total

            def one_copy(p, _):
                gather_copy(m, p).start()
                return 0

            lax.fori_loop(1, TILES, one_copy, 0, unroll=9)

        for m in range(MODES):
            gather(m)

        more = it < ITERS - 1
        share = remote(gobj.at[0, k], gobj.at[0, k], s_share, r_share, t, other)
        for j in range(3):
            cols = slice(j * L, (j + 1) * L)
            for i in ((0, 2, 5), (1, 3, 6), (4,))[j]:
                margin_sends[i].wait()
            upper = g_own[j, 0:N] + m_below[j].astype(F32)
            lower = g_own[j, N:TILE]
            if j < 2:
                upper = upper + m_diag[j].astype(F32) + m_right[j, 0:N].astype(F32)
                lower = lower + m_right[j, N:TILE].astype(F32)
            gobj[0, k, 0:N, cols] = upper.astype(BF16)
            gobj[0, k, N:TILE, cols] = lower.astype(BF16)

            @pl.when(more)
            def _():
                now = objs[k, :, cols] - STEP_OBJECT * gobj[0, k, :, cols].astype(F32)
                objs[k, :, cols] = now
                ob[j] = now.astype(BF16)
                for i in ((5, 2, 0), (6, 3, 1), (4,))[j]:
                    halo_sends[i].start()

        share.start()

        for m in range(MODES):
            whole = rs_recv.at[m, pl.ds(16, 63 * 16)]
            remote(whole, whole, s_ag.at[m], r_ag.at[m], away(1), k).wait()
        share.wait()

        @pl.when(more)
        def _():
            probes[...] = probes[...] - STEP_PROBE * gprobe[...].astype(F32)
            objs[other] = objs[other] - STEP_OBJECT * gobj[0, other].astype(F32)

        return 0

    lax.fori_loop(0, ITERS, sweep, 0)


def body(obj, probe, mode_weights, measured, corner, counts, weight_index):
    vmem = pl.BlockSpec(memory_space=pltpu.VMEM)
    smem = pl.BlockSpec(memory_space=pltpu.SMEM)
    hbm = pl.BlockSpec(memory_space=pl.ANY)
    dma = pltpu.SemaphoreType.DMA
    regular = pltpu.SemaphoreType.REGULAR
    obj_1, grad_obj, probe_1, grad_probe = pl.pallas_call(
        kernel,
        name="ptycho",
        out_shape=(
            pltpu.VMEM(obj.shape, F32),
            pltpu.VMEM(obj.shape, BF16),
            pltpu.VMEM(probe.shape, F32),
            pltpu.VMEM(probe.shape, BF16),
        ),
        in_specs=[hbm, hbm, smem, hbm, smem, smem, smem, hbm, hbm],
        out_specs=(vmem, vmem, vmem, vmem),
        scratch_shapes=[
            pltpu.VMEM((SLOTS, N, N), F32),
            pltpu.VMEM((2 * N, 2 * N), BF16),
            pltpu.VMEM((2 * N, 2 * N), BF16),
            pltpu.VMEM((2, 5, FRAME, L), F32),
            pltpu.VMEM((3, TILE, L), BF16),
            pltpu.VMEM((2, 2, TILE, L), BF16),
            pltpu.VMEM((2, 3, N, L), BF16),
            pltpu.VMEM((2, 2, N, L), BF16),
            pltpu.VMEM((SLOTS, 2, N, N), F32),
            pltpu.VMEM((SLOTS, MODES, N, 2 * N), F32),
            pltpu.VMEM((SLOTS, N, N), F32),
            pltpu.VMEM((SLOTS, N, N), BF16),
            pltpu.VMEM((SLOTS, N, N), BF16),
            pltpu.VMEM((SLOTS, 2, N, N), F32),
            pltpu.VMEM((2, N, N), F32),
            pltpu.VMEM((25, 1024, L), F32),
            pltpu.VMEM((5, FRAME, L), BF16),
            pltpu.VMEM((5, FRAME, L), BF16),
            pltpu.VMEM((3, TILE, L), F32),
            pltpu.VMEM((5, FRAME, L), BF16),
            pltpu.VMEM((2, TILE, L), BF16),
            pltpu.VMEM((3, N, L), BF16),
            pltpu.VMEM((2, N, L), BF16),
            pltpu.VMEM((MODES, 2, N, N), BF16),
            pltpu.VMEM((MODES, 1024, L), BF16),
            pltpu.VMEM((MODES, 16, L), BF16),
            dma((5,)), dma((7,)), dma((7,)), dma((7,)), dma((7,)), dma((4,)), dma((4,)),
            dma((2,)), dma((2,)), dma((7,)), dma((7,)),
            dma((2,)), dma((2,)), dma((2,)), dma((2,)), dma, dma, regular, regular,
        ],
        compiler_params=pltpu.CompilerParams(
            collective_id=0, has_side_effects=True, vmem_limit_bytes=54 << 20
        ),
    )(obj, probe, mode_weights.T, measured, corner.T, counts, weight_index, *dft_tables())
    return (
        obj_1 - STEP_OBJECT * grad_obj.astype(F32),
        probe_1 - STEP_PROBE * grad_probe.astype(F32),
    )


def solution(mesh):
    placed = (
        P("tile", None, None, None),
        P("mode", None, None, None),
        P(None, "mode"),
        P("tile", None, None),
        P("tile", None),
        P("tile"),
        P("tile"),
    )
    return jax.shard_map(
        body,
        mesh=mesh,
        in_specs=placed,
        out_specs=(P("tile", None, None, None), P("mode", None, None, None)),
        check_vma=False,
    )
```

```python
import functools

import jax
import jax.numpy as jnp
import numpy as np
from jax import lax
from jax.experimental import pallas as pl
from jax.experimental.pallas import tpu as pltpu
from jax.sharding import PartitionSpec as P

MESH = pl.DeviceIdType.MESH
BF16 = jnp.bfloat16
F32 = jnp.float32
GC = 8
ITERS = 2
TILES = 64
SLOTS = 4
MODES = 2
N = 256
L = 128
TILE = 384
FRAME = 640
STEP_OBJECT = 0.1
STEP_PROBE = 4.0 / 128.0


def dft_tables():
    index = np.arange(N, dtype=np.int64)
    angle = (index[:, None] * index[None, :] % N).astype(np.float32) * np.float32(2.0 * np.pi / N)
    factor = np.float32(1.0 / 16.0)
    real = np.cos(angle) * factor
    imag = -np.sin(angle) * factor
    one = np.block([[real, -imag], [imag, real]])
    two = np.block([[real, imag], [-imag, real]])
    return jnp.asarray(one, BF16), jnp.asarray(two, BF16)


def transform(fields, left, right):
    stacked = jnp.concatenate([jnp.concatenate(pair, 0) for pair in fields], 1)
    first = jnp.dot(left[...], stacked, preferred_element_type=F32).astype(BF16)
    rows = [
        jnp.concatenate([first[:N, i * N:(i + 1) * N], first[N:, i * N:(i + 1) * N]], 1)
        for i in range(len(fields))
    ]
    second = jnp.dot(jnp.concatenate(rows, 0), right[...], preferred_element_type=F32)
    return [second[i * N:(i + 1) * N] for i in range(len(fields))]


def kernel(
    obj_hbm, probe_hbm, mw_ref, meas_hbm, corner_ref, counts_ref, widx_ref, one_hbm, two_hbm,
    obj_out, gobj, probe_out, gprobe,
    meas, one, two,
    frame, ob, h_right, h_below, h_diag,
    patches, psi, inten, ipart_s, ipart_r, terms, pgrad, zall,
    g_send, g_recv, g_own, margin, m_right, m_below, m_diag,
    rs_send, rs_recv, ag_mine,
    s_in, s_halo, r_halo, s_fwd, r_fwd, s_int, r_int, s_g, r_g, s_m, r_m,
    s_rs, r_rs, s_ag, r_ag, s_share, r_share, stage_y, stage_z,
):
    objs = obj_out.at[0]
    probes = probe_out
    t = lax.axis_index("tile")
    k = lax.axis_index("mode")
    other = 1 - k

    def away(by):
        return lax.rem(t + (TILES + by) % TILES, TILES)

    def along(axis, by):
        size = 4 ** axis
        digit = lax.rem(lax.div(t, size), 4)
        return t + (lax.rem(digit + by, 4) - digit) * size

    def remote(src, dst, ssem, rsem, tile, core):
        return pltpu.make_async_remote_copy(
            src_ref=src, dst_ref=dst, send_sem=ssem, recv_sem=rsem,
            device_id=(tile, core), device_id_type=MESH,
        )

    def signal(sem, tile, core):
        pl.semaphore_signal(sem, inc=1, device_id=(tile, core), device_id_type=MESH)

    loads = [
        pltpu.make_async_copy(src, dst, s_in.at[i])
        for i, (src, dst) in enumerate(
            ((obj_hbm.at[0], objs), (probe_hbm, probes), (one_hbm, one), (two_hbm, two), (meas_hbm, meas))
        )
    ]
    loads[0].start()

    barrier = pltpu.get_barrier_semaphore()
    signal(barrier, t, other)
    for by in (1, GC, GC + 1):
        signal(barrier, away(by), k)
        signal(barrier, away(-by), k)
    for axis in range(3):
        for by in (1, 2, 3):
            signal(barrier, along(axis, by), k)
    for load in loads[1:]:
        load.start()

    loads[0].wait()
    for j in range(3):
        ob[j] = objs[k, :, j * L:(j + 1) * L].astype(BF16)
    pl.semaphore_wait(barrier, 16)

    lane = lax.broadcasted_iota(jnp.int32, (N, L), 1)

    def halo_chunks():
        for j in range(2):
            yield ob.at[j], h_right.at[k, j], away(-1)
        for j in range(3):
            yield ob.at[j, pl.ds(0, N)], h_below.at[k, j], away(-GC)
        for j in range(2):
            yield ob.at[j, pl.ds(0, N)], h_diag.at[k, j], away(-GC - 1)

    halo_sends = [
        remote(src, dst, s_halo.at[i], r_halo.at[i], to, k)
        for i, (src, dst, to) in enumerate(halo_chunks())
    ]
    halo_forwards = [
        remote(dst, dst, s_fwd.at[i], r_fwd.at[i], t, other)
        for i, (src, dst, to) in enumerate(halo_chunks())
    ]
    halo_order = (5, 6, 2, 3, 4, 0, 1)

    def margin_chunks():
        for j in range(2):
            yield margin.at[3 + j, pl.ds(0, TILE)], m_right.at[j], away(1)
        for j in range(3):
            yield margin.at[j, pl.ds(TILE, N)], m_below.at[j], away(GC)
        for j in range(2):
            yield margin.at[3 + j, pl.ds(TILE, N)], m_diag.at[j], away(GC + 1)

    margin_sends = [
        remote(src, dst, s_m.at[i], r_m.at[i], to, k)
        for i, (src, dst, to) in enumerate(margin_chunks())
    ]

    for i in halo_order:
        halo_sends[i].start()

    for by in (1, 2, 3):
        signal(stage_y, along(0, by), k)
    zall[0] = jnp.zeros((1024, L), F32)

    def clear(i, _):
        zall[i, 0:TILE] = jnp.zeros((TILE, L), F32)
        zall[i, FRAME:1024] = jnp.zeros((1024 - FRAME, L), F32)
        return 0

    lax.fori_loop(1, 13, clear, 0)
    pl.semaphore_wait(stage_y, 3)
    for by in (1, 2, 3):
        signal(stage_z, along(2, by), k)
    lax.fori_loop(13, 25, clear, 0)
    pl.semaphore_wait(stage_z, 3)
    for load in loads[1:]:
        load.wait()

    def shard(ref, m, tile):
        return ref.at[
            m, lax.div(tile, 32),
            pl.ds(pl.multiple_of(lax.rem(tile, 16) * 16, 16), 16),
            pl.ds(pl.multiple_of(lax.rem(lax.div(tile, 16), 2) * L, L), L),
        ]

    def sweep(it, _):
        for c in range(2):
            for j in range(3):
                frame[c, j, 0:TILE] = objs[c, :, j * L:(j + 1) * L].astype(BF16).astype(F32)
        for i in halo_order:
            halo_sends[i].wait_recv()
            halo_forwards[i].start()

        def settle(c):
            for j in range(2):
                frame[c, 3 + j, 0:TILE] = h_right[c, j].astype(F32)
            for j in range(3):
                frame[c, j, TILE:FRAME] = h_below[c, j].astype(F32)
            for j in range(2):
                frame[c, 3 + j, TILE:FRAME] = h_diag[c, j].astype(F32)

        settle(k)
        for i in halo_order:
            halo_forwards[i].wait()
        settle(other)
        for send in halo_sends:
            send.wait_send()

        def intensity_copy(s):
            return remote(ipart_s.at[s], ipart_r.at[s], s_int.at[s], r_int.at[s], t, other)

        def forward_slot(s):
            row = corner_ref[0, s]
            col = corner_ref[1, s]
            q = lax.div(col, L)
            rem = lax.rem(col, L)
            back = lax.rem(L - rem, L)
            for c in range(2):
                rolled = [
                    pltpu.roll(frame[c, q + j, pl.ds(row, N), :], back, 1) for j in range(3)
                ]
                for j in range(2):
                    patches[s, c, :, j * L:(j + 1) * L] = jnp.where(
                        lane < L - rem, rolled[j], rolled[j + 1]
                    )
            o_re = patches[s, 0]
            o_im = patches[s, 1]
            fields = []
            for m in range(MODES):
                p_re = probes[m, 0]
                p_im = probes[m, 1]
                e_re = (p_re * o_re - p_im * o_im).astype(BF16)
                e_im = (p_re * o_im + p_im * o_re).astype(BF16)
                fields.append((e_re, e_im))
            total = None
            for m, wave in enumerate(transform(fields, one, two)):
                psi[s, m] = wave
                w = mw_ref[m, widx_ref[s]]
                part = w * (wave[:, :N] * wave[:, :N] + wave[:, N:] * wave[:, N:])
                total = part if total is None else total + part
            inten[s] = total
            ipart_s[s] = total.astype(BF16)
            intensity_copy(s).start()

        def forward_pair(i, _):
            forward_slot(2 * i)
            forward_slot(2 * i + 1)
            return 0

        lax.fori_loop(0, SLOTS // 2, forward_pair, 0)

        def scatter_copy(m, p):
            peer = lax.rem(t + 21 * p, TILES)
            return remote(
                shard(rs_send, m, peer), rs_recv.at[m, pl.ds(p * 16, 16)],
                s_rs.at[m], r_rs.at[m], peer, k,
            )

        def gather_copy(m, p):
            peer = lax.rem(t + 21 * p, TILES)
            return remote(
                ag_mine.at[m], shard(gprobe, m, t), s_ag.at[m], r_ag.at[m], peer, k
            )

        for m in range(MODES):
            pgrad[...] = jnp.zeros_like(pgrad)

            def backward_pair(i):
                fields = []
                for s in (2 * i, 2 * i + 1):
                    w = mw_ref[m, widx_ref[s]]
                    if m == 0:
                        intensity_copy(s).wait()
                        live = jnp.where(s < counts_ref[0], 1.0, 0.0).astype(F32)
                        inten[s] = (inten[s] + ipart_r[s].astype(F32) - meas[s]) * live
                    factor = w * inten[s]
                    s_re = (factor * psi[s, m, :, 0:N]).astype(BF16)
                    s_im = (factor * psi[s, m, :, N:2 * N]).astype(BF16)
                    fields.append((s_re, s_im))
                p_re = probes[m, 0]
                p_im = probes[m, 1]
                for s, chi in zip((2 * i, 2 * i + 1), transform(fields, two, one)):
                    c_re = chi[:, :N]
                    c_im = chi[:, N:]
                    o_re = patches[s, 0]
                    o_im = patches[s, 1]
                    t_re = p_re * c_re + p_im * c_im
                    t_im = p_re * c_im - p_im * c_re
                    if m == 0:
                        terms[s, 0] = t_re
                        terms[s, 1] = t_im
                    else:
                        terms[s, 0] = terms[s, 0] + t_re
                        terms[s, 1] = terms[s, 1] + t_im
                    pgrad[0] = pgrad[0] + o_re * c_re + o_im * c_im
                    pgrad[1] = pgrad[1] + o_re * c_im - o_im * c_re

            def backward_step(i, _):
                backward_pair(i)
                return 0

            lax.fori_loop(0, SLOTS // 2, backward_step, 0)
            rs_send[m] = pgrad[...].astype(BF16)

            def scatter(p, _):
                scatter_copy(m, p).start()
                return 0

            lax.fori_loop(1, TILES, scatter, 0, unroll=9)

        def spread(s, _):
            rem = lax.rem(corner_ref[1, s], L)
            for c in range(2):
                left = pltpu.roll(terms[s, c, :, 0:L], rem, 1)
                right = pltpu.roll(terms[s, c, :, L:2 * L], rem, 1)
                base = 1 + (s * 2 + c) * 3
                zall[base, TILE:FRAME] = jnp.where(lane >= rem, left, 0.0)
                zall[base + 1, TILE:FRAME] = jnp.where(lane >= rem, right, left)
                zall[base + 2, TILE:FRAME] = jnp.where(lane >= rem, 0.0, right)
            return 0

        lax.fori_loop(0, SLOTS, spread, 0)

        rows_block = 128

        def place(c, j, b):
            total = None
            for s in range(SLOTS):
                d = j - lax.div(corner_ref[1, s], L)
                inside = jnp.logical_and(d >= 0, d <= 2)
                index = jnp.where(inside, 1 + (s * 2 + c) * 3 + d, 0)
                start = TILE - corner_ref[0, s] + b * rows_block
                part = zall[index, pl.ds(start, rows_block), :]
                total = part if total is None else total + part
            return total

        def block(b):
            return pl.ds(pl.multiple_of(b * rows_block, rows_block), rows_block)

        def place_send(i, _):
            j = lax.div(i, 5)
            b = lax.rem(i, 5)
            g_send[j, block(b), :] = place(other, j, b).astype(BF16)
            return 0

        pairs = [
            remote(g_send.at[js], g_recv.at[js], s_g.at[i], r_g.at[i], t, other)
            for i, js in enumerate((pl.ds(3, 2), pl.ds(0, 3)))
        ]
        lax.fori_loop(15, 25, place_send, 0)
        pairs[0].start()
        lax.fori_loop(0, 15, place_send, 0)
        pairs[1].start()

        def place_margin(j, b):
            margin[j, block(b), :] = (
                place(k, j, b) + g_recv[j, block(b), :].astype(F32)
            ).astype(BF16)

        def place_right(i, _):
            place_margin(3 + lax.div(i, 5), lax.rem(i, 5))
            return 0

        def place_below(i, _):
            place_margin(lax.div(i, 2), 3 + lax.rem(i, 2))
            return 0

        def place_tile(i, _):
            j = lax.div(i, 3)
            b = lax.rem(i, 3)
            g_own[j, block(b), :] = place(k, j, b) + g_recv[j, block(b), :].astype(F32)
            return 0

        pairs[0].wait()
        lax.fori_loop(0, 10, place_right, 0)
        for i in (5, 6, 0, 1):
            margin_sends[i].start()
        pairs[1].wait()
        lax.fori_loop(0, 6, place_below, 0)
        for i in (2, 3, 4):
            margin_sends[i].start()
        lax.fori_loop(0, 9, place_tile, 0)

        def gather(m):
            whole = rs_recv.at[m, pl.ds(16, 63 * 16)]
            remote(whole, whole, s_rs.at[m], r_rs.at[m], away(1), k).wait()
            own = shard(rs_send, m, t)[...].astype(F32)
            rest = rs_recv[m, 16:64 * 16].astype(F32).reshape(63, 16, L)
            total = (own + jnp.sum(rest, 0)).astype(BF16)
            ag_mine[m] = total
            shard(gprobe, m, t)[...] = total

            def one_copy(p, _):
                gather_copy(m, p).start()
                return 0

            lax.fori_loop(1, TILES, one_copy, 0, unroll=9)

        for m in range(MODES):
            gather(m)

        more = it < ITERS - 1
        share = remote(gobj.at[0, k], gobj.at[0, k], s_share, r_share, t, other)
        for j in range(3):
            cols = slice(j * L, (j + 1) * L)
            for i in ((0, 2, 5), (1, 3, 6), (4,))[j]:
                margin_sends[i].wait()
            upper = g_own[j, 0:N] + m_below[j].astype(F32)
            lower = g_own[j, N:TILE]
            if j < 2:
                upper = upper + m_diag[j].astype(F32) + m_right[j, 0:N].astype(F32)
                lower = lower + m_right[j, N:TILE].astype(F32)
            gobj[0, k, 0:N, cols] = upper.astype(BF16)
            gobj[0, k, N:TILE, cols] = lower.astype(BF16)

            @pl.when(more)
            def _():
                now = objs[k, :, cols] - STEP_OBJECT * gobj[0, k, :, cols].astype(F32)
                objs[k, :, cols] = now
                ob[j] = now.astype(BF16)
                for i in ((5, 2, 0), (6, 3, 1), (4,))[j]:
                    halo_sends[i].start()

        share.start()

        for m in range(MODES):
            whole = rs_recv.at[m, pl.ds(16, 63 * 16)]
            remote(whole, whole, s_ag.at[m], r_ag.at[m], away(1), k).wait()
        share.wait()

        @pl.when(more)
        def _():
            probes[...] = probes[...] - STEP_PROBE * gprobe[...].astype(F32)
            objs[other] = objs[other] - STEP_OBJECT * gobj[0, other].astype(F32)

        return 0

    lax.fori_loop(0, ITERS, sweep, 0)


def body(obj, probe, mode_weights, measured, corner, counts, weight_index):
    vmem = pl.BlockSpec(memory_space=pltpu.VMEM)
    smem = pl.BlockSpec(memory_space=pltpu.SMEM)
    hbm = pl.BlockSpec(memory_space=pl.ANY)
    dma = pltpu.SemaphoreType.DMA
    regular = pltpu.SemaphoreType.REGULAR
    obj_1, grad_obj, probe_1, grad_probe = pl.pallas_call(
        kernel,
        name="ptycho",
        out_shape=(
            pltpu.VMEM(obj.shape, F32),
            pltpu.VMEM(obj.shape, BF16),
            pltpu.VMEM(probe.shape, F32),
            pltpu.VMEM(probe.shape, BF16),
        ),
        in_specs=[hbm, hbm, smem, hbm, smem, smem, smem, hbm, hbm],
        out_specs=(vmem, vmem, vmem, vmem),
        scratch_shapes=[
            pltpu.VMEM((SLOTS, N, N), F32),
            pltpu.VMEM((2 * N, 2 * N), BF16),
            pltpu.VMEM((2 * N, 2 * N), BF16),
            pltpu.VMEM((2, 5, FRAME, L), F32),
            pltpu.VMEM((3, TILE, L), BF16),
            pltpu.VMEM((2, 2, TILE, L), BF16),
            pltpu.VMEM((2, 3, N, L), BF16),
            pltpu.VMEM((2, 2, N, L), BF16),
            pltpu.VMEM((SLOTS, 2, N, N), F32),
            pltpu.VMEM((SLOTS, MODES, N, 2 * N), F32),
            pltpu.VMEM((SLOTS, N, N), F32),
            pltpu.VMEM((SLOTS, N, N), BF16),
            pltpu.VMEM((SLOTS, N, N), BF16),
            pltpu.VMEM((SLOTS, 2, N, N), F32),
            pltpu.VMEM((2, N, N), F32),
            pltpu.VMEM((25, 1024, L), F32),
            pltpu.VMEM((5, FRAME, L), BF16),
            pltpu.VMEM((5, FRAME, L), BF16),
            pltpu.VMEM((3, TILE, L), F32),
            pltpu.VMEM((5, FRAME, L), BF16),
            pltpu.VMEM((2, TILE, L), BF16),
            pltpu.VMEM((3, N, L), BF16),
            pltpu.VMEM((2, N, L), BF16),
            pltpu.VMEM((MODES, 2, N, N), BF16),
            pltpu.VMEM((MODES, 1024, L), BF16),
            pltpu.VMEM((MODES, 16, L), BF16),
            dma((5,)), dma((7,)), dma((7,)), dma((7,)), dma((7,)), dma((4,)), dma((4,)),
            dma((2,)), dma((2,)), dma((7,)), dma((7,)),
            dma((2,)), dma((2,)), dma((2,)), dma((2,)), dma, dma, regular, regular,
        ],
        compiler_params=pltpu.CompilerParams(
            collective_id=0, has_side_effects=True, vmem_limit_bytes=54 << 20
        ),
    )(obj, probe, mode_weights.T, measured, corner.T, counts, weight_index, *dft_tables())
    return (
        obj_1 - STEP_OBJECT * grad_obj.astype(F32),
        probe_1 - STEP_PROBE * grad_probe.astype(F32),
    )


def solution(mesh):
    placed = (
        P("tile", None, None, None),
        P("mode", None, None, None),
        P(None, "mode"),
        P("tile", None, None),
        P("tile", None),
        P("tile"),
        P("tile"),
    )
    return jax.shard_map(
        body,
        mesh=mesh,
        in_specs=placed,
        out_specs=(P("tile", None, None, None), P("mode", None, None, None)),
        check_vma=False,
    )
```
